512 devices in a mesh: dp: 32 (over z, core), vocab: 16 (over y, x).
Axes of the slice: x: 4, y: 4, z: 16, core: 2. Of those that a mesh axis runs over, the one named last changes fastest.
Arguments:
- hidden: bfloat16 [640, 12288], P(None, 'dp'), may hold values from -4 to 4
- table: bfloat16 [32768, 12288], P('vocab', 'dp'), may hold values from -1.2 to 1.2
- targets: int32 [640], replicated, may hold values from 0 to 32767
- owners: int32 [640, 1], replicated, may hold values from 0 to 15; in each aligned block of 40 rows (0 to 39, 40 to 79, ...) at most 10 rows name the same one
- rows: int32 [640], replicated, may hold values from 0 to 2047
- input_grad: bfloat16 [640, 12288], P('vocab', 'dp'), may hold values from -6 to 6
Outputs:
- token_loss: float32 [640], P('dp')
- hidden_grad: bfloat16 [640, 12288], P('vocab', 'dp')
- table_grad: float32 [32768, 12288], P('vocab', 'dp')
The draws below stay inside these ranges and needn't reach their ends.
Inputs may be any that keep to these rules, and one draw needn't show every extreme that they name: `owners`: in each aligned block of 40 tokens, no owner is named more than 10 times, a bound that some block reaches.
All inputs are finite; a program needn't handle non-finite values.
Results may differ from the reference program's by a relative error of at most 0.0034.
Values may be sent and summed in bfloat16 or wider, within the bound.
A program may use at most 64 MiB of HBM per device.

```python
import math
import jax
import jax.numpy as jnp
import numpy as np
from jax import lax

D = 12288
V_DEV = 2048
TOKENS = 640
V = 32768
CAP = 10
N_VOCAB = 16


logit_scale = 0.8333333


def table_values(key, indices):

    def single(row_number):
        return jax.random.normal(jax.random.fold_in(key, row_number), (D,), jnp.float32)
    return jnp.clip(0.2 * jax.vmap(single)(indices), -1.2, 1.2)


def draw_table(key, part):
    return table_values(key, jnp.arange(V, dtype=jnp.int32)).astype(jnp.bfloat16)


def aligned_rows(base_key, key):
    picked = jax.random.randint(jax.random.fold_in(key, 4), (3, 2), 0, V)
    first_rows = table_values(base_key, picked[:, 0])
    second_rows = table_values(base_key, picked[:, 1])
    strength = jnp.array([140.0, 200.0, 260.0], jnp.float32)
    factor = strength / (logit_scale * 0.04 * D)
    return factor[:, None] * (first_rows + (1.0 - 2.0 / strength)[:, None] * second_rows)


def draw_hidden(key, part):
    base_key = key
    key = jax.random.fold_in(key, 3)
    aligned = aligned_rows(base_key, key)
    values = 0.2 * jax.random.normal(jax.random.fold_in(key, 2), (TOKENS, D), jnp.float32)
    values = jnp.concatenate([aligned, values[3:]], axis=0)
    return jnp.clip(values, -4.0, 4.0).astype(jnp.bfloat16)


def plant(result, rng, least, top_value):
    dims = result.shape
    index_at = [jax.random.randint(jax.random.fold_in(rng, axis), (), 0, dims[axis]) for axis in range(len(dims))]
    result = result.at[tuple(index_at)].set(least)
    longest = dims.index(max(dims))
    index_at[longest] = (index_at[longest] + 1) % dims[longest]
    return result.at[tuple(index_at)].set(top_value)


def levels(rng, shape, split, low, top_value):
    def one(position, blocks):
        heights = jax.random.uniform(jax.random.fold_in(jax.random.fold_in(rng, 6), position), (blocks,), jnp.float32, low / len(split), top_value / len(split))
        return jnp.repeat(jnp.exp(heights), shape[position] // blocks).reshape((-1,) + (1,) * (len(shape) - position - 1))

    factor_of = one(*split[0])
    for cut in split[1:]:
        factor_of = factor_of * one(*cut)
    return factor_of


def rank_table(number_of, lean):
    weights = [(1 << 20) // math.isqrt(standing ** lean) + 1 for standing in range(1, number_of + 1)]
    scale = 1 + sum(weights) // (1 << 30)
    return np.cumsum(np.array([max(1, weight // scale) for weight in weights]))


def skewed_ids(stream_key, shape, number_of, skew):
    listing = rank_table(number_of, skew)
    pick = jax.random.randint(jax.random.fold_in(stream_key, 1), shape, 0, int(listing[number_of - 1]))
    rank = jnp.searchsorted(jnp.asarray(listing, jnp.int32), pick, side="right")
    return jax.random.permutation(jax.random.fold_in(stream_key, 2), number_of)[rank].astype(jnp.int32)


def deal_out(rng, own, number, rows, count, top, bound, skew):
    order = jax.random.permutation(rng, count)
    packed, ordinary = portions_of(count, rows * top, bound, skew, True), portions_of(count, rows * top, bound, skew, False)
    places = jnp.arange(count)

    def named(lengths, offset_by):
        used = int((lengths > 0).sum())
        fixed = max(1, used // 4)
        moved = fixed + (places - fixed + offset_by * (used - fixed)) % max(1, count - fixed)
        return jnp.zeros((count,), jnp.int32).at[order[jnp.where(places < fixed, places, moved)]].set(jnp.asarray(lengths, jnp.int32))

    lengths = jnp.where(number % 4 == 0, named(packed, number // 4), named(ordinary, number - number // 4 - 1))
    mixed = jax.random.permutation(jax.random.fold_in(own, 3), count)
    source_of, sink = mixed[0:count // 2 * 2:2], mixed[1:count // 2 * 2:2]
    margin = jnp.minimum(lengths[source_of] - 1, bound - lengths[sink]) // 2
    margin = jnp.where((source_of == order[0]) | (sink == order[0]) | (lengths[sink] == 0), 0, jnp.maximum(margin, 0))
    moved = jax.random.randint(jax.random.fold_in(own, 4), (count // 2,), 0, 1 << 20) % (margin + 1)
    lengths = lengths.at[source_of].add(-moved).at[sink].add(moved)
    items = jnp.searchsorted(jnp.cumsum(lengths), jnp.arange(rows * top), side="right").astype(jnp.int32)
    grid = items.reshape(top, rows).T
    grid = grid[jax.random.permutation(jax.random.fold_in(own, 1), rows)]
    offset_by = jax.random.randint(jax.random.fold_in(own, 2), (rows, 1), 0, top)
    return jnp.take_along_axis(grid, (jnp.arange(top)[None, :] + offset_by) % top, axis=1)


def portions_of(count, total, limit, skew, full):
    weights = [(1 << 20) // math.isqrt(standing ** skew) + 1 for standing in range(1, count + 1)]
    largest = limit if full else min(limit, max(-(-total // count), total * weights[0] // sum(weights)))
    least = 1 if total - largest >= count - 1 else 0
    given, spare = [largest] + [least] * (count - 1), total - largest - least * (count - 1)
    while spare > 0:
        movable = [i for i in range(1, count) if given[i] < largest] or [i for i in range(1, count) if given[i] < limit]
        mass, budget = sum([weights[i] for i in movable]), spare
        for i in movable:
            more = min(limit - given[i], max(1, budget * weights[i] // mass), spare)
            given[i] = given[i] + more
            spare = spare - more
    return np.array(given)


def normal_values(own_key, extent, scale, limit, split=(), kind=jnp.bfloat16):
    drawn = scale * jax.random.normal(own_key, extent, jnp.float32)
    if split:
        drawn = drawn * levels(own_key, extent, split, -0.22, 0.18)
    return jnp.clip(drawn, -limit, limit).astype(kind)


def setup_inputs(seed: int = 0) -> dict:
    seeds = jax.random.split(jax.random.key(seed), 7)
    hidden = draw_hidden(jax.random.fold_in(seeds[6], 71), 0)
    table = draw_table(jax.random.fold_in(seeds[6], 71), 0)
    targets = plant(skewed_ids(seeds[2], (TOKENS,), V, 2), jax.random.fold_in(seeds[2], 3), 0, V - 1).astype(jnp.int32)
    owners_keys = jax.random.split(jax.random.fold_in(seeds[3], 1), TOKENS // (TOKENS // N_VOCAB))
    owners_turns = jax.random.permutation(jax.random.fold_in(seeds[3], 3), TOKENS // (TOKENS // N_VOCAB))
    owners = jax.vmap(lambda own, number: deal_out(jax.random.fold_in(seeds[3], 2), own, number, TOKENS // N_VOCAB, N_VOCAB, 1, CAP, 2))(owners_keys, owners_turns).reshape((TOKENS, 1))
    rows = plant(skewed_ids(seeds[4], (TOKENS,), V_DEV, 2), jax.random.fold_in(seeds[4], 3), 0, V_DEV - 1).astype(jnp.int32)
    input_grad = normal_values(seeds[5], (TOKENS, D), 1.0, 6.0, ((0, 16), (1, 32)))
    return dict(hidden=hidden, table=table, targets=targets, owners=owners, rows=rows, input_grad=input_grad)


logit_scale = 0.8333333

def reference(hidden, table, targets, owners, rows, input_grad):
    logits = logit_scale * lax.dot_general(hidden, table, (((1,), (1,)), ((), ())), preferred_element_type=jnp.float32)
    highest = lax.optimization_barrier(jnp.max(logits, axis=1))
    log_total = highest + jnp.log(lax.optimization_barrier(jnp.sum(jnp.exp(logits - highest[:, None]), axis=1)))
    columns = jnp.arange(V, dtype=jnp.int32)
    aimed = targets[:, None] == columns[None, :]
    target_logit = lax.optimization_barrier(jnp.sum(jnp.where(aimed, logits, 0.0), axis=1))
    token_loss = log_total - target_logit
    grads = (jnp.exp(logits - log_total[:, None]) - aimed.astype(jnp.float32)).astype(jnp.bfloat16)
    hidden_grad = (logit_scale * jnp.dot(grads, table, preferred_element_type=jnp.float32)).astype(jnp.bfloat16)
    ids = (owners[:, 0] * V_DEV + rows).astype(jnp.int32)
    chosen = (ids[:, None] == columns[None, :]).astype(jnp.bfloat16)

    def block_grad(block):
        start = (block * V_DEV).astype(jnp.int32)
        part_grads = lax.dynamic_slice_in_dim(grads, start, V_DEV, 1)
        part_chosen = lax.dynamic_slice_in_dim(chosen, start, V_DEV, 1)
        head = lax.dot_general(part_grads, hidden, (((0,), (0,)), ((), ())), preferred_element_type=jnp.float32)
        embed = lax.dot_general(part_chosen, input_grad, (((0,), (0,)), ((), ())), preferred_element_type=jnp.float32)
        return logit_scale * head + embed
    table_grad = lax.map(block_grad, jnp.arange(N_VOCAB, dtype=jnp.int32)).reshape(V, D)
    return (token_loss, hidden_grad, table_grad)
```

```python
import functools

import jax
import jax.numpy as jnp
from jax import lax
from jax.experimental import pallas as pl
from jax.experimental.pallas import tpu as pltpu
from jax.sharding import PartitionSpec as P

logit_scale = 0.8333333
MESH = pl.DeviceIdType.MESH
LANES = 128
PHASES = ((0, 24), (24, 16))
SKEW = 2
CHUNKS = 4


def head_kernel(
    nz, nv,
    targets_ref, rows_ref, owners_ref, ig_ref, hidden_hbm, table_hbm,
    loss_ref, hg_ref, tg_hbm,
    hidc, tabc, tab, part, ring_a, ring_b, lg_a, lg_b, g_all, gn_a, gn_b, acc,
    hgs_a, hgs_b, hgr_a, hgr_b, igs, st1_a, st1_b, st2_a, st2_b,
    load_sem, give_send, give_recv, rs_send, rs_recv, ag_send, ag_recv, core_send, core_recv,
    st1_send, st1_recv, st2_send, st2_recv, ig_send, ig_recv, hg_send, hg_recv, out_sem,
):
    half_ring = nz // 2
    tokens, width = hidden_hbm.shape
    vocab_part = table_hbm.shape[0]
    half = vocab_part // 2
    quarter = half // 2
    block = tokens // nz
    ring = (ring_a, ring_b)
    lg = (lg_a, lg_b)
    gn = (gn_a, gn_b)
    hgs = (hgs_a, hgs_b)
    hgr = (hgr_a, hgr_b)
    st1 = (st1_a, st1_b)
    st2 = (st2_a, st2_b)
    dp = lax.axis_index("dp")
    v = lax.axis_index("vocab")
    z = dp // 2
    c = dp % 2
    near = {"dp": z * 2 + (1 - c)}
    step_to = tuple({"dp": ((z + nz + sign) % nz) * 2 + c} for sign in (1, -1))
    signs = (1, -1)

    def at_z(offset):
        return (z + offset + 2 * nz) % nz

    def peer(i):
        return (v + i) % nv

    def remote(src, dst, send, recv, device):
        return pltpu.make_async_remote_copy(
            src_ref=src, dst_ref=dst, send_sem=send, recv_sem=recv,
            device_id=device, device_id_type=MESH,
        )

    my_lanes = pl.ds(pl.multiple_of(c * width, LANES), width)
    my_half = pl.ds(pl.multiple_of(c * half, half), half)
    loads = [
        pltpu.make_async_copy(hidden_hbm, hidc.at[:, my_lanes], load_sem.at[0]),
        pltpu.make_async_copy(table_hbm.at[my_half], tabc.at[:, my_lanes], load_sem.at[1]),
        pltpu.make_async_copy(table_hbm, tab, load_sem.at[2]),
    ]
    for copy in loads:
        copy.start()
    barrier = pltpu.get_barrier_semaphore()
    for device in (near, step_to[0], step_to[1]):
        pl.semaphore_signal(barrier, inc=1, device_id=device, device_id_type=MESH)

    @pl.loop(1, nv)
    def _(i):
        pl.semaphore_signal(barrier, inc=1, device_id={"vocab": peer(i)}, device_id_type=MESH)

    pl.semaphore_wait(barrier, 3 + nv - 1)

    chunk = half // CHUNKS
    gives = [remote(hidden_hbm, hidc.at[:, my_lanes], give_send.at[0], give_recv.at[0], near)]
    for j in range(CHUNKS):
        its = pl.ds(pl.multiple_of((1 - c) * half + j * chunk, chunk), chunk)
        gives.append(
            remote(
                table_hbm.at[its],
                tabc.at[pl.ds(j * chunk, chunk), my_lanes],
                give_send.at[1 + j],
                give_recv.at[1 + j],
                near,
            )
        )
    for copy in gives:
        copy.start()
    sent = list(gives)

    def rs_copy(p, h, way, s):
        first, count = PHASES[p]
        cols = pl.ds(h * quarter, quarter)
        return remote(
            part.at[at_z(signs[way] * (half_ring - s)), pl.ds(first, count), cols],
            ring[p].at[way, s, :, cols],
            rs_send.at[p, h, way, s],
            rs_recv.at[p, h, way, s],
            step_to[way],
        )

    def rs_exists(h, way, s):
        return s > 0 or h == way

    def rs_start(p, h, way, s):
        copy = rs_copy(p, h, way, s)
        copy.start()
        sent.append(copy)

    def rs_advance(p, h, way, s):
        first, count = PHASES[p]
        if rs_exists(h, way, s):
            rs_copy(p, h, way, s).wait_recv()
            d = at_z(signs[way] * (half_ring - 1 - s))
            spot = (d, pl.ds(first, count), pl.ds(h * quarter, quarter))
            part[spot] = part[spot] + ring[p][way, s, :, h * quarter : (h + 1) * quarter]
        if s + 1 < half_ring:
            rs_start(p, h, way, s + 1)

    def rs_step(p, s):
        for h in range(2):
            for way in range(2):
                if rs_exists(h, way, s):
                    rs_advance(p, h, way, s)

    loads[0].wait()
    loads[1].wait()
    gives[0].wait_recv()
    for j in range(CHUNKS):
        gives[1 + j].wait_recv()
        cols = slice(j * chunk, (j + 1) * chunk)
        part[:, :, cols] = lax.dot_general(
            hidc[...], tabc[cols, :], (((1,), (1,)), ((), ())),
            preferred_element_type=jnp.float32,
        ).reshape(nz, block, chunk)
        if j == CHUNKS // 2 - 1:
            rs_start(0, 0, 0, 0)
    rs_start(0, 1, 1, 0)
    if half_ring > 1:
        rs_start(0, 1, 0, 1)
        rs_start(0, 0, 1, 1)

    def rs_open(p):
        rs_start(p, 0, 0, 0)
        rs_start(p, 1, 1, 0)
        if half_ring > 1:
            rs_start(p, 1, 0, 1)
            rs_start(p, 0, 1, 1)

    igs[v] = ig_ref[...].astype(jnp.float32)

    def ig_copy(i):
        to = peer(i)
        return remote(igs.at[v], igs.at[v], ig_send.at[i], ig_recv.at[i], {"vocab": to})

    @pl.loop(1, nv)
    def _(i):
        ig_copy(i).start()

    def wait_ig():
        @pl.loop(1, nv)
        def _(i):
            ig_copy(i).wait_recv()

    piece = vocab_part // 8

    def embed(j):
        ids = owners_ref[...] * vocab_part + rows_ref[...] - (v * vocab_part + j * piece)
        chosen = (lax.broadcasted_iota(jnp.int32, (piece, tokens), 0) == ids).astype(jnp.float32)
        acc[pl.ds(j * piece, piece), :] = jnp.dot(
            chosen.astype(jnp.bfloat16),
            igs[...].reshape(tokens, width).astype(jnp.bfloat16),
            preferred_element_type=jnp.float32,
        )

    lane = lax.broadcasted_iota(jnp.int32, (1, LANES), 1)

    def aimed_of(p):
        first, count = PHASES[p]
        token = lax.broadcasted_iota(jnp.int32, (count, tokens), 0) + (z * block + first)
        here = lax.broadcasted_iota(jnp.int32, (count, tokens), 1) == token
        wanted = jnp.sum(
            jnp.where(here, targets_ref[...].astype(jnp.float32), 0.0), axis=1, keepdims=True
        ).astype(jnp.int32)
        column = lax.broadcasted_iota(jnp.int32, (count, half), 1) + (v * vocab_part + c * half)
        return column == wanted

    def st1_copy(p):
        return remote(st1[p].at[0], st1[p].at[1], st1_send.at[p], st1_recv.at[p], near)

    def st2_copy(p, i):
        return remote(
            st2[p].at[v], st2[p].at[v], st2_send.at[p, i], st2_recv.at[p, i], {"vocab": peer(i)}
        )

    def pack(m, s, t):
        return jnp.where(lane == 0, m, jnp.where(lane == 1, s, t))

    def stats_local(p):
        first, count = PHASES[p]
        last = half_ring - 1
        for h in range(2):
            for way in range(2):
                if rs_exists(h, way, last):
                    rs_copy(p, h, way, last).wait_recv()
        total = part[z, pl.ds(first, count), :]
        if last > 0:
            total = total + ring[p][0, last] + ring[p][1, last]
            x = logit_scale * total
            lg[p][...] = x
        else:
            lg[p][:, :quarter] = logit_scale * (total[:, :quarter] + ring[p][0, 0, :, :quarter])
            lg[p][:, quarter:] = logit_scale * (total[:, quarter:] + ring[p][1, 0, :, quarter:])
            x = lg[p][...]
        m = jnp.max(x, axis=1, keepdims=True)
        s = jnp.sum(jnp.exp(x - m), axis=1, keepdims=True)
        t = jnp.sum(jnp.where(aimed_of(p), x, 0.0), axis=1, keepdims=True)
        st1[p][0] = pack(m, s, t)
        st1_copy(p).start()

    def stats_core(p):
        st1_copy(p).wait_recv()
        one, two = st1[p][0], st1[p][1]
        m1, m2 = one[:, 0:1], two[:, 0:1]
        m = jnp.maximum(m1, m2)
        s = one[:, 1:2] * jnp.exp(m1 - m) + two[:, 1:2] * jnp.exp(m2 - m)
        st2[p][v] = pack(m, s, one[:, 2:3] + two[:, 2:3])

        @pl.loop(1, nv)
        def _(i):
            st2_copy(p, i).start()

    def stats_final(p):
        first, count = PHASES[p]

        @pl.loop(1, nv)
        def _(i):
            st2_copy(p, i).wait_recv()

        every = st2[p][...]
        m, s, t = every[:, :, 0:1], every[:, :, 1:2], every[:, :, 2:3]
        top = jnp.max(m, axis=0)
        log_total = top + jnp.log(jnp.sum(s * jnp.exp(m - top[None]), axis=0))
        loss_ref[pl.ds(first, count), :] = jnp.broadcast_to(
            log_total - jnp.sum(t, axis=0), (count, LANES)
        )
        grads = jnp.exp(lg[p][...] - log_total) - aimed_of(p).astype(jnp.float32)
        for g in range(count // 8):
            eight = grads[g * 8 : (g + 1) * 8]
            g_all[c, z, first // 8 + g] = jnp.concatenate(
                [eight[:, :quarter], eight[:, quarter:]], axis=0
            ).astype(jnp.bfloat16)

    def ag_copy(p, way, s):
        first, count = PHASES[p]
        d = at_z(-signs[way] * s)
        groups = pl.ds(first // 8, count // 8)
        lanes = pl.ds(0, quarter)
        if s == half_ring - 1:
            lanes = pl.ds(way * (quarter // 2), quarter // 2)
        ref = g_all.at[c, d, groups, :, lanes]
        return remote(ref, ref, ag_send.at[p, way, s], ag_recv.at[p, way, s], step_to[way])

    def core_copy(p, k, d, side):
        first, count = PHASES[p]
        ref = g_all.at[side, d, pl.ds(first // 8, count // 8)]
        return remote(ref, ref, core_send.at[p, k], core_recv.at[p, k], near)

    def core_block(k):
        if k == 0:
            return z
        if k == nz - 1:
            return at_z(half_ring)
        return at_z(-signs[(k - 1) % 2] * ((k - 1) // 2 + 1))

    def core_start(p, k):
        copy = core_copy(p, k, core_block(k), c)
        copy.start()
        sent.append(copy)

    def ag_start(p, way, s):
        copy = ag_copy(p, way, s)
        copy.start()
        sent.append(copy)

    def ag_open(p):
        for way in range(2):
            ag_start(p, way, 0)
        core_start(p, 0)

    def ag_step(p, s):
        for way in range(2):
            ag_copy(p, way, s).wait_recv()
            if s + 1 < half_ring:
                ag_start(p, way, s + 1)
                core_start(p, 1 + 2 * s + way)
        if s + 1 == half_ring:
            core_start(p, nz - 1)

    def ag_close(p):
        first, count = PHASES[p]
        for k in range(nz):
            core_copy(p, k, core_block(k), 1 - c).wait_recv()
        for side in range(2):
            x = g_all[side, :, first // 8 : (first + count) // 8].astype(jnp.float32)
            for part_of in range(2):
                cols = slice(side * half + part_of * quarter, side * half + (part_of + 1) * quarter)
                gn[p][:, cols] = (
                    x[:, :, 8 * part_of : 8 * part_of + 8, :]
                    .reshape(nz * count, quarter)
                    .astype(jnp.bfloat16)
                )

    def hg_copy(p, i):
        to = peer(i)
        return remote(
            hgs[p].at[to], hgr[p].at[v], hg_send.at[p, i], hg_recv.at[p, i], {"vocab": to}
        )

    def hg_start(p):
        count = PHASES[p][1]
        hgs[p][...] = jnp.dot(
            gn[p][...], tab[...], preferred_element_type=jnp.float32
        ).reshape(nv, count, width)
        hgr[p][v] = hgs[p][v]

        @pl.loop(1, nv)
        def _(i):
            hg_copy(p, i).start()

    def hg_wait(p):
        @pl.loop(1, nv)
        def _(i):
            hg_copy(p, i).wait_recv()

    def hidden_rows(p):
        first, count = PHASES[p]
        own = hidc[:, my_lanes].astype(jnp.float32).reshape(nz, block, width)
        return own[:, first : first + count].reshape(nz * count, width).astype(jnp.bfloat16)

    def head(p, j, own):
        spot = (pl.ds(j * piece, piece), slice(None))
        acc[spot] = acc[spot] + logit_scale * lax.dot_general(
            gn[p][:, j * piece : (j + 1) * piece], own, (((0,), (0,)), ((), ())),
            preferred_element_type=jnp.float32,
        )

    def out_copy(j):
        rows = pl.ds(j * piece, piece)
        return pltpu.make_async_copy(acc.at[rows], tg_hbm.at[rows], out_sem.at[j])

    filler = [functools.partial(embed, j) for j in range(8)]
    for slot in range(half_ring - 1 + SKEW):
        if slot < half_ring - 1:
            rs_step(0, slot)
        elif slot == half_ring - 1:
            stats_local(0)
        if slot == SKEW:
            rs_open(1)
        if slot >= SKEW:
            rs_step(1, slot - SKEW)
        if slot == half_ring:
            stats_core(0)
        if slot == 1:
            wait_ig()
        if slot >= 1 and filler:
            filler.pop(0)()
            if slot >= 2 and filler:
                filler.pop(0)()
    while filler:
        filler.pop(0)()
    if SKEW < 1:
        stats_local(0)
    if SKEW < 2:
        stats_core(0)
    stats_local(1)
    stats_final(0)
    ag_open(0)
    stats_core(1)
    for s in range(half_ring):
        ag_step(0, s)
        if s == min(1, half_ring - 1):
            stats_final(1)
            ag_open(1)
        if s >= 2:
            ag_step(1, s - 2)
    loads[2].wait()
    own = hidden_rows(0)
    for s in range(max(half_ring - 2, 0), half_ring):
        ag_step(1, s)
        if s == max(half_ring - 2, 0):
            ag_close(0)
            hg_start(0)
    for j in range(8):
        head(0, j, own)
    ag_close(1)
    hg_start(1)
    own = hidden_rows(1)
    for j in range(8):
        head(1, j, own)
        out_copy(j).start()
    for p in range(2):
        hg_wait(p)
    pieces = []
    for p in range(2):
        pieces.append(jnp.sum(hgr[p][...], axis=0))
    hg_ref[...] = (logit_scale * jnp.concatenate(pieces, axis=0)).astype(jnp.bfloat16)

    for copy in sent:
        copy.wait_send()
    for p in range(2):
        st1_copy(p).wait_send()

    @pl.loop(1, nv)
    def _(i):
        ig_copy(i).wait_send()
        for p in range(2):
            st2_copy(p, i).wait_send()
            hg_copy(p, i).wait_send()

    for j in range(8):
        out_copy(j).wait()


def on_device(hidden, table, targets, owners, rows, input_grad):
    nz = lax.axis_size("dp") // 2
    nv = lax.axis_size("vocab")
    tokens, width = hidden.shape
    vocab_part = table.shape[0]
    half = vocab_part // 2
    block = tokens // nz
    half_ring = nz // 2
    counts = [count for _, count in PHASES]
    f32, bf16 = jnp.float32, jnp.bfloat16
    vmem = pl.BlockSpec(memory_space=pltpu.VMEM)
    hbm = pl.BlockSpec(memory_space=pl.ANY)
    dma = pltpu.SemaphoreType.DMA
    each = lambda shape, kind: [pltpu.VMEM(shape(count), kind) for count in counts]
    loss, hidden_grad, table_grad = pl.pallas_call(
        functools.partial(head_kernel, nz, nv),
        out_shape=(
            jax.ShapeDtypeStruct((block, LANES), f32),
            jax.ShapeDtypeStruct((block, width), bf16),
            jax.ShapeDtypeStruct((vocab_part, width), f32),
        ),
        in_specs=[vmem, vmem, vmem, vmem, hbm, hbm],
        out_specs=(vmem, vmem, hbm),
        scratch_shapes=[
            pltpu.VMEM((tokens, 2 * width), bf16),
            pltpu.VMEM((half, 2 * width), bf16),
            pltpu.VMEM((vocab_part, width), bf16),
            pltpu.VMEM((nz, block, half), f32),
            *each(lambda n: (2, half_ring, n, half), f32),
            *each(lambda n: (n, half), f32),
            pltpu.VMEM((2, nz, block // 8, 16, half // 2), bf16),
            *each(lambda n: (nz * n, vocab_part), bf16),
            pltpu.VMEM((vocab_part, width), f32),
            *each(lambda n: (nv, n, width), f32),
            *each(lambda n: (nv, n, width), f32),
            pltpu.VMEM((nv, block, width), f32),
            *each(lambda n: (2, n, LANES), f32),
            *each(lambda n: (nv, n, LANES), f32),
            dma((3,)),
            dma((1 + CHUNKS,)),
            dma((1 + CHUNKS,)),
            dma((2, 2, 2, half_ring)),
            dma((2, 2, 2, half_ring)),
            dma((2, 2, half_ring)),
            dma((2, 2, half_ring)),
            dma((2, nz)),
            dma((2, nz)),
            dma((2,)),
            dma((2,)),
            dma((2, nv)),
            dma((2, nv)),
            dma((nv,)),
            dma((nv,)),
            dma((2, nv)),
            dma((2, nv)),
            dma((8,)),
        ],
        compiler_params=pltpu.CompilerParams(
            collective_id=0, has_side_effects=True, vmem_limit_bytes=56 * 1024 * 1024
        ),
        name="head",
    )(
        targets.reshape(1, tokens), rows.reshape(1, tokens), owners.reshape(1, tokens),
        input_grad, hidden, table,
    )
    token_loss = lax.dynamic_slice(
        loss[:, 0], ((lax.axis_index("dp") % 2) * (block // 2),), (block // 2,)
    )
    return (token_loss, hidden_grad, table_grad)


def solution(mesh):
    return jax.shard_map(
        on_device,
        mesh=mesh,
        in_specs=(P(None, "dp"), P("vocab", "dp"), P(), P(), P(), P("vocab", "dp")),
        out_specs=(P("dp"), P("vocab", "dp"), P("vocab", "dp")),
        check_vma=False,
    )
```

```python
import functools

import jax
import jax.numpy as jnp
from jax import lax
from jax.experimental import pallas as pl
from jax.experimental.pallas import tpu as pltpu
from jax.sharding import PartitionSpec as P

logit_scale = 0.8333333
MESH = pl.DeviceIdType.MESH
LANES = 128
CHUNKS = 4
PAD = 8
PIECES = 8
AG_TREE = {7: 5}
AG_ORDER = (1, 2, 3, 4, 5, 6, 7, 8)


def head_kernel(
    nz, nv,
    targets_ref, rows_ref, owners_ref, ig_ref, hidden_hbm, table_hbm,
    loss_ref, hg_ref, tg_hbm,
    hidc, tabc, tab, part, ring, g_all, gn, acc, hid32, hid_near, tcol,
    hgs, hgr, igs, mst, st1, st2, stz,
    load_sem, give_send, give_recv, rs_send, rs_recv, ag_send, ag_recv, core_send, core_recv,
    st1_send, st1_recv, st2_send, st2_recv, stz_send, stz_recv, ig_send, ig_recv,
    hg_send, hg_recv, out_sem,
):
    half_ring = nz // 2
    tree = {b: AG_TREE.get(b, b - 1) if nz == 16 else b - 1 for b in range(1, half_ring + 1)}
    tokens, width = hidden_hbm.shape
    vocab_part = table_hbm.shape[0]
    half = vocab_part // 2
    quarter = half // 2
    block = tokens // nz
    groups = block // 8
    dp = lax.axis_index("dp")
    v = lax.axis_index("vocab")
    z = dp // 2
    c = dp % 2
    signs = (1, -1)

    def at_z(offset):
        return (z + offset + 2 * nz) % nz

    def peer(i):
        return (v + i) % nv

    def zdev(offset):
        return {"dp": at_z(offset) * 2 + c}

    near = {"dp": z * 2 + (1 - c)}
    step_to = tuple(zdev(sign) for sign in signs)

    def nearby(k):
        return at_z(jnp.where(k % 2 == 1, -((k + 1) // 2), k // 2))

    def remote(src, dst, send, recv, device):
        return pltpu.make_async_remote_copy(
            src_ref=src, dst_ref=dst, send_sem=send, recv_sem=recv,
            device_id=device, device_id_type=MESH,
        )

    my_lanes = pl.ds(pl.multiple_of(c * width, LANES), width)
    my_half = pl.ds(pl.multiple_of(c * half, half), half)
    loads = [
        pltpu.make_async_copy(hidden_hbm, hidc.at[:, my_lanes], load_sem.at[0]),
        pltpu.make_async_copy(table_hbm.at[my_half], tabc.at[:, my_lanes], load_sem.at[1]),
        pltpu.make_async_copy(table_hbm, tab, load_sem.at[2]),
    ]
    barrier = pltpu.get_barrier_semaphore()
    pl.semaphore_signal(barrier, inc=1, device_id=near, device_id_type=MESH)
    for copy in loads:
        copy.start()

    @pl.loop(1, nz)
    def _(i):
        pl.semaphore_signal(barrier, inc=1, device_id=zdev(i), device_id_type=MESH)

    @pl.loop(1, nv)
    def _(i):
        pl.semaphore_signal(barrier, inc=1, device_id={"vocab": peer(i)}, device_id_type=MESH)

    pl.semaphore_wait(barrier, nz + nv - 1)

    chunk = half // CHUNKS
    gives = [remote(hidden_hbm, hidc.at[:, my_lanes], give_send.at[0], give_recv.at[0], near)]
    for j in range(CHUNKS):
        its = pl.ds(pl.multiple_of((1 - c) * half + j * chunk, chunk), chunk)
        gives.append(
            remote(
                table_hbm.at[its],
                tabc.at[pl.ds(j * chunk, chunk), my_lanes],
                give_send.at[1 + j],
                give_recv.at[1 + j],
                near,
            )
        )
    for copy in gives:
        copy.start()

    def rs_copy(way, s, g):
        rows = pl.ds(pl.multiple_of(g * 8, 8), 8)
        cols = pl.ds(0, half) if s else pl.ds(way * quarter, quarter)
        return remote(
            part.at[at_z(signs[way] * (half_ring - s)), rows, cols],
            ring.at[way, s, rows, cols],
            rs_send.at[way, min(s, 1)],
            rs_recv.at[way, s, g],
            step_to[way],
        )

    def rs_open(way):
        @pl.loop(0, groups)
        def _(g):
            rs_copy(way, 0, g).start()

    def rs_step(s):
        @pl.loop(0, groups)
        def _(g):
            rows = pl.ds(pl.multiple_of(g * 8, 8), 8)
            for way in range(2):
                cols = pl.ds(0, half) if s else pl.ds(way * quarter, quarter)
                rs_copy(way, s, g).wait_recv()
                spot = (at_z(signs[way] * (half_ring - 1 - s)), rows, cols)
                part[spot] = part[spot] + ring[way, s, rows, cols]
                rs_copy(way, s + 1, g).start()

    loads[0].wait()
    loads[1].wait()
    gives[0].wait_recv()
    for j in range(CHUNKS):
        gives[1 + j].wait_recv()
        cols = slice(j * chunk, (j + 1) * chunk)
        part[:, :, cols] = lax.dot_general(
            hidc[...], tabc[cols, :], (((1,), (1,)), ((), ())),
            preferred_element_type=jnp.float32,
        ).reshape(nz, block, chunk)
        if j == CHUNKS // 2 - 1:
            rs_open(0)
    rs_open(1)

    igs[v] = ig_ref[...].astype(jnp.float32)

    def ig_copy(i):
        return remote(igs.at[v], igs.at[v], ig_send, ig_recv, {"vocab": peer(i)})

    @pl.loop(1, nv)
    def _(i):
        ig_copy(i).start()

    def wait_ig():
        rest = igs.at[pl.ds(1, nv - 1)]
        remote(rest, rest, ig_send, ig_recv, near).wait_recv()

    piece = vocab_part // 8

    def embed(j):
        ids = owners_ref[...] * vocab_part + rows_ref[...].reshape(1, tokens) - (v * vocab_part + j * piece)
        chosen = (lax.broadcasted_iota(jnp.int32, (piece, tokens), 0) == ids).astype(jnp.float32)
        acc[pl.ds(j * piece, piece), :] = jnp.dot(
            chosen.astype(jnp.bfloat16),
            igs[...].reshape(tokens, width).astype(jnp.bfloat16),
            preferred_element_type=jnp.float32,
        )

    def own_rows():
        hid32[...] = hidc[:, my_lanes].astype(jnp.float32).reshape(nz, block, width)

    def pair_rows():
        @pl.loop(0, nz // 2)
        def _(j):
            two = jnp.concatenate([hid32[nearby(2 * j)], hid32[nearby(2 * j + 1)]], axis=0)
            rows = pl.ds(pl.multiple_of(j * 2 * block, 16), 2 * block)
            hid_near[rows, :] = two.astype(jnp.bfloat16)

    def target_columns():
        @pl.loop(0, nz)
        def _(d):
            token = lax.broadcasted_iota(jnp.int32, (block, tokens), 0) + d * block
            here = lax.broadcasted_iota(jnp.int32, (block, tokens), 1) == token
            wanted = jnp.sum(
                jnp.where(here, targets_ref[...].reshape(1, tokens).astype(jnp.float32), 0.0), axis=1, keepdims=True
            )
            tcol[d] = jnp.broadcast_to(wanted.astype(jnp.int32), (block, LANES))

    lane = lax.broadcasted_iota(jnp.int32, (1, LANES), 1)
    sub = lax.broadcasted_iota(jnp.int32, (8, LANES), 0)
    eye = lax.broadcasted_iota(jnp.int32, (block, LANES), 0) == lax.broadcasted_iota(
        jnp.int32, (block, LANES), 1
    )
    first_col = v * vocab_part

    def as_row(x):
        return jnp.sum(jnp.where(eye, x, 0.0), axis=0, keepdims=True)

    def as_col(x):
        return jnp.sum(jnp.where(eye, x, 0.0), axis=1, keepdims=True)

    st1_copy = remote(st1.at[0], st1.at[1], st1_send, st1_recv, near)

    def st2_copy(i):
        return remote(st2.at[v], st2.at[v], st2_send, st2_recv, {"vocab": peer(i)})

    def stz_copy(i):
        return remote(stz.at[z], stz.at[z], stz_send, stz_recv, zdev(i))

    def pack(a, b, c):
        return jnp.where(sub == 0, a, jnp.where(sub == 1, b, c))

    def ag_copy(way, b, g):
        a = tree[b]
        d = at_z(-signs[way] * a)
        lanes = pl.ds(0, quarter)
        if b == half_ring:
            lanes = pl.ds(way * (quarter // 2), quarter // 2)
        ref = g_all.at[c, d, g, :, lanes]
        return remote(
            ref, ref, ag_send.at[way, b // half_ring], ag_recv.at[way, b - 1, g],
            zdev(signs[way] * (b - a)),
        )

    def ag_on(way, a, g):
        for b in sorted(tree):
            if tree[b] == a:
                ag_copy(way, b, g).start()

    def core_copy(k, side):
        ref = g_all.at[side, nearby(k)]
        return remote(ref, ref, core_send, core_recv.at[k], near)

    def ag_step(b):
        @pl.loop(0, groups)
        def _(g):
            for way in range(2):
                ag_copy(way, b, g).wait_recv()
                ag_on(way, b, g)

        core_copy(2 * b - 1, c).start()
        if b < half_ring:
            core_copy(2 * b, c).start()

    def finish_logits():
        last = half_ring - 1

        @pl.loop(0, groups)
        def _(g):
            rows = pl.ds(pl.multiple_of(g * 8, 8), 8)
            for way in range(2):
                rs_copy(way, last, g).wait_recv()
            x = logit_scale * (part[z, rows, :] + ring[0, last, rows, :] + ring[1, last, rows, :])
            m = jnp.max(x, axis=1, keepdims=True)
            e = jnp.exp(x - m)
            g_all[c, z, g] = jnp.concatenate([e[:, :quarter], e[:, quarter:]], axis=0).astype(
                jnp.bfloat16
            )
            for way in range(2):
                ag_on(way, 0, g)
            column = lax.broadcasted_iota(jnp.int32, (8, half), 1) + (first_col + c * half)
            aimed = column == tcol[z, rows, 0:1]
            t = jnp.sum(jnp.where(aimed, x, 0.0), axis=1, keepdims=True)
            mst[rows, :] = jnp.where(
                lane == 0, m, jnp.where(lane == 1, jnp.sum(e, axis=1, keepdims=True), t)
            )

        st1[0] = pack(as_row(mst[:, 0:1]), as_row(mst[:, 1:2]), as_row(mst[:, 2:3]))
        st1_copy.start()
        core_copy(0, c).start()

    def stats_core():
        st1_copy.wait_recv()
        one, two = st1[0], st1[1]
        m1, m2 = one[0:1], two[0:1]
        m = jnp.maximum(m1, m2)
        s = one[1:2] * jnp.exp(m1 - m) + two[1:2] * jnp.exp(m2 - m)
        st2[v] = pack(m, s, one[2:3] + two[2:3])

        @pl.loop(1, nv)
        def _(i):
            st2_copy(i).start()

    def stats_final():
        rest = st2.at[pl.ds(1, nv - 1)]
        remote(rest, rest, st2_send, st2_recv, near).wait_recv()

        every = st2[...]
        m, s, t = every[:, 0], every[:, 1], every[:, 2]
        top = jnp.max(m, axis=0, keepdims=True)
        log_total = top + jnp.log(jnp.sum(s * jnp.exp(m - top), axis=0, keepdims=True))
        target = jnp.sum(t, axis=0, keepdims=True)
        mine = jnp.exp(st1[0, 0:1, :] - log_total)
        other = jnp.exp(st1[1, 0:1, :] - log_total)
        stz[z] = pack(
            jnp.where(c == 0, mine, other),
            jnp.where(c == 0, other, mine),
            jnp.exp(target - log_total) - 1.0,
        )

        @pl.loop(1, nz)
        def _(i):
            stz_copy(i).start()

        pick = lax.broadcasted_iota(jnp.int32, (block, LANES), 0) == (
            lax.broadcasted_iota(jnp.int32, (block, LANES), 1) + c * (block // 2)
        )
        loss_ref[...] = jnp.broadcast_to(
            jnp.sum(jnp.where(pick, as_col(log_total - target), 0.0), axis=0, keepdims=True),
            (8, LANES),
        )

    def stz_wait():
        rest = stz.at[pl.ds(1, nz - 1)]
        remote(rest, rest, stz_send, stz_recv, near).wait_recv()

    def core_wait(first, last):
        for k in range(first, last):
            core_copy(k, 1 - c).wait_recv()

    def gradients(first, last):
        @pl.loop(first // 2, last // 2)
        def _(j):
            rows = pl.ds(pl.multiple_of(j * 2 * block, 16), 2 * block)
            ds = [nearby(2 * j), nearby(2 * j + 1)]
            factors = [[as_col(stz[d, r : r + 1, :]) for r in range(3)] for d in ds]
            wanted = [tcol[d, :, 0:1] - first_col for d in ds]
            for side in range(2):
                for q in range(2):
                    base = side * half + q * quarter
                    column = lax.broadcasted_iota(jnp.int32, (block, quarter), 1) + base
                    both = []
                    for d, f, w in zip(ds, factors, wanted):
                        e = g_all[side, d].astype(jnp.float32)[:, 8 * q : 8 * q + 8, :]
                        both.append(
                            jnp.where(column == w, f[2], e.reshape(block, quarter) * f[side])
                        )
                    gn[rows, base : base + quarter] = jnp.concatenate(both, axis=0).astype(
                        jnp.bfloat16
                    )

    def hg_copy(k):
        to = nearby(k)
        return remote(
            hgs.at[k], hgr.at[v], hg_send, hg_recv, {"vocab": to}
        )

    def hidden_terms(first, last):
        if first == last:
            return
        terms = jnp.dot(
            gn[first * block : last * block, :], tab[...], preferred_element_type=jnp.float32
        ).reshape(last - first, block, width)
        low = jnp.concatenate([terms, jnp.zeros((last - first, PAD, width), jnp.float32)], axis=1)
        hgs[first:last] = low.astype(jnp.bfloat16)

        @pl.loop(first, last)
        def _(k):
            @pl.when(nearby(k) != v)
            def _():
                hg_copy(k).start()

    def hg_finish():
        offset = (v - z + nz + half_ring) % nz - half_ring
        k = jnp.where(offset < 0, -2 * offset - 1, 2 * offset)
        hgr[v] = hgs[k]

        rest = hgr.at[pl.ds(1, nv - 1)]
        remote(rest, rest, hg_send, hg_recv, near).wait_recv()
        hg_ref[...] = (
            logit_scale * jnp.sum(hgr[...].astype(jnp.float32)[:, :block], axis=0)
        ).astype(jnp.bfloat16)

    def head(j):
        spot = (pl.ds(j * piece, piece), slice(None))
        acc[spot] = acc[spot] + logit_scale * lax.dot_general(
            gn[:, j * piece : (j + 1) * piece], hid_near[...], (((0,), (0,)), ((), ())),
            preferred_element_type=jnp.float32,
        )

    def out_copy(j):
        rows = pl.ds(j * piece, piece)
        return pltpu.make_async_copy(acc.at[rows], tg_hbm.at[rows], out_sem.at[j])

    filler = [target_columns, own_rows, pair_rows, wait_ig]
    filler = filler + [functools.partial(embed, j) for j in range(8)]
    for s in range(half_ring - 1):
        rs_step(s)
        for _ in range(2):
            if filler:
                filler.pop(0)()
    while filler:
        filler.pop(0)()
    loads[2].wait()
    finish_logits()
    third = 3 * nz // 8 * 2
    stats_core()
    todo = {
        2: [stats_final],
        5: [stz_wait, lambda: core_wait(0, nz // 2), lambda: gradients(0, nz // 2)],
        7: [
            lambda: hidden_terms(0, nz // 2),
            lambda: core_wait(nz // 2, third),
            lambda: gradients(nz // 2, third),
        ],
    }
    for b in AG_ORDER if nz == 16 else range(1, half_ring + 1):
        ag_step(b)
        for act in todo.pop(b, []):
            act()
    for b in sorted(todo):
        for act in todo[b]:
            act()
    hidden_terms(nz // 2, third)
    core_wait(third, nz)
    gradients(third, nz)
    hidden_terms(third, nz)
    for j in range(8):
        head(j)
        out_copy(j).start()
    hg_finish()

    for copy in gives:
        copy.wait_send()
    st1_copy.wait_send()

    def all_sent(ref, sem):
        remote(ref, ref, sem, sem, near).wait_send()

    for way in range(2):
        all_sent(ring.at[way, 0, :, pl.ds(0, quarter)], rs_send.at[way, 0])
        all_sent(ring.at[way, pl.ds(1, half_ring - 1)], rs_send.at[way, 1])
        all_sent(g_all.at[c, pl.ds(1, half_ring - 1)], ag_send.at[way, 0])
        all_sent(g_all.at[c, 0, :, :, pl.ds(0, quarter // 2)], ag_send.at[way, 1])
    all_sent(g_all.at[c], core_send)
    all_sent(igs.at[pl.ds(1, nv - 1)], ig_send)
    all_sent(st2.at[pl.ds(1, nv - 1)], st2_send)
    all_sent(stz.at[pl.ds(1, nz - 1)], stz_send)
    all_sent(hgs.at[pl.ds(1, nv - 1)], hg_send)
    for j in range(8):
        out_copy(j).wait()


def hand_over(loss_ref, hg_in, tg_in, loss_out, hg_out, tg_out, held, in_sem, out_sem):
    def copies(j):
        spot = pl.ds(j * (tg_in.shape[0] // PIECES), tg_in.shape[0] // PIECES)
        return (
            pltpu.make_async_copy(tg_in.at[spot], held.at[spot], in_sem.at[j]),
            pltpu.make_async_copy(held.at[spot], tg_out.at[spot], out_sem.at[j]),
        )

    for j in range(PIECES):
        copies(j)[0].start()
    loss_out[...] = loss_ref[0:1, : loss_out.shape[1]]
    hg_out[...] = hg_in[...]
    for j in range(PIECES):
        copies(j)[0].wait()
        copies(j)[1].start()
    for j in range(PIECES):
        copies(j)[1].wait()


def on_device(hidden, table, targets, owners, rows, input_grad):
    nz = lax.axis_size("dp") // 2
    nv = lax.axis_size("vocab")
    tokens, width = hidden.shape
    vocab_part = table.shape[0]
    half = vocab_part // 2
    block = tokens // nz
    groups = block // 8
    half_ring = nz // 2
    f32, bf16 = jnp.float32, jnp.bfloat16
    vmem = pl.BlockSpec(memory_space=pltpu.VMEM)
    hbm = pl.BlockSpec(memory_space=pl.ANY)
    dma = pltpu.SemaphoreType.DMA
    loss, hidden_grad, table_grad = pl.pallas_call(
        functools.partial(head_kernel, nz, nv),
        out_shape=(
            jax.ShapeDtypeStruct((8, LANES), f32),
            jax.ShapeDtypeStruct((block, width), bf16),
            jax.ShapeDtypeStruct((vocab_part, width), f32),
        ),
        in_specs=[vmem, vmem, vmem, vmem, hbm, hbm],
        out_specs=(vmem, vmem, hbm),
        scratch_shapes=[
            pltpu.VMEM((tokens, 2 * width), bf16),
            pltpu.VMEM((half, 2 * width), bf16),
            pltpu.VMEM((vocab_part, width), bf16),
            pltpu.VMEM((nz, block, half), f32),
            pltpu.VMEM((2, half_ring, block, half), f32),
            pltpu.VMEM((2, nz, groups, 16, half // 2), bf16),
            pltpu.VMEM((tokens, vocab_part), bf16),
            pltpu.VMEM((vocab_part, width), f32),
            pltpu.VMEM((nz, block, width), f32),
            pltpu.VMEM((tokens, width), bf16),
            pltpu.VMEM((nz, block, LANES), jnp.int32),
            pltpu.VMEM((nz, block + PAD, width), bf16),
            pltpu.VMEM((nv, block + PAD, width), bf16),
            pltpu.VMEM((nv, block, width), f32),
            pltpu.VMEM((block, LANES), f32),
            pltpu.VMEM((2, 8, LANES), f32),
            pltpu.VMEM((nv, 8, LANES), f32),
            pltpu.VMEM((nz, 8, LANES), f32),
            dma((3,)),
            dma((1 + CHUNKS,)),
            dma((1 + CHUNKS,)),
            dma((2, 2)),
            dma((2, half_ring, groups)),
            dma((2, 2)),
            dma((2, half_ring, groups)),
            dma,
            dma((nz,)),
            *[dma] * 10,
            dma((8,)),
        ],
        compiler_params=pltpu.CompilerParams(
            collective_id=0, has_side_effects=True, vmem_limit_bytes=58 * 1024 * 1024
        ),
        name="head",
    )(
        targets, rows, owners.reshape(1, tokens),
        input_grad, hidden, table,
    )
    token_loss, hidden_grad, table_grad = pl.pallas_call(
        hand_over,
        out_shape=(
            jax.ShapeDtypeStruct((1, block // 2), f32),
            jax.ShapeDtypeStruct((block, width), bf16),
            jax.ShapeDtypeStruct((vocab_part, width), f32),
        ),
        in_specs=[vmem, vmem, hbm],
        out_specs=(vmem, vmem, hbm),
        scratch_shapes=[pltpu.VMEM((vocab_part, width), f32), dma((PIECES,)), dma((PIECES,))],
        compiler_params=pltpu.CompilerParams(vmem_limit_bytes=58 * 1024 * 1024),
        name="hand_over",
    )(loss, hidden_grad, table_grad)
    return (token_loss.reshape(block // 2), hidden_grad, table_grad)


def solution(mesh):
    return jax.shard_map(
        on_device,
        mesh=mesh,
        in_specs=(P(None, "dp"), P("vocab", "dp"), P(), P(), P(), P("vocab", "dp")),
        out_specs=(P("dp"), P("vocab", "dp"), P("vocab", "dp")),
        check_vma=False,
    )
```

```python
import functools

import jax
import jax.numpy as jnp
from jax import lax
from jax.experimental import pallas as pl
from jax.experimental.pallas import tpu as pltpu
from jax.sharding import PartitionSpec as P

logit_scale = 0.8333333
MESH = pl.DeviceIdType.MESH
LANES = 128
CHUNKS = 4
PIECES = 8
AG_TREE = {7: 5}
AG_ORDER = (1, 2, 3, 4, 5, 6, 7, 8)


def head_kernel(
    nz, nv,
    targets_ref, rows_ref, owners_ref, ig_ref, hidden_hbm, table_hbm,
    loss_ref, hg_ref, tg_hbm,
    hidc, tabc, tab, part, ring, g_all, gn, acc, hid32, hid_near, tcol,
    hgs, hgr, igs, mst, st1, st2, stz,
    load_sem, give_send, give_recv, rs_send, rs_recv, ag_send, ag_recv, core_send, core_recv,
    st1_send, st1_recv, st2_send, st2_recv, stz_send, stz_recv, ig_send, ig_recv,
    hg_send, hg_recv, cross_send, cross_recv, pass_send, pass_recv, out_sem,
):
    half_ring = nz // 2
    tree = {b: AG_TREE.get(b, b - 1) if nz == 16 else b - 1 for b in range(1, half_ring + 1)}
    tokens, width = hidden_hbm.shape
    vocab_part = table_hbm.shape[0]
    half = vocab_part // 2
    quarter = half // 2
    block = tokens // nz
    groups = block // 8
    dp = lax.axis_index("dp")
    v = lax.axis_index("vocab")
    z = dp // 2
    c = dp % 2
    signs = (1, -1)

    def at_z(offset):
        return (z + offset + 2 * nz) % nz

    def peer(i):
        return (v + i) % nv

    def zdev(offset):
        return {"dp": at_z(offset) * 2 + c}

    near = {"dp": z * 2 + (1 - c)}
    step_to = tuple(zdev(sign) for sign in signs)
    cross_to = tuple({"dp": at_z(sign) * 2 + (1 - c)} for sign in signs)

    def nearby(k):
        return at_z(jnp.where(k % 2 == 1, -((k + 1) // 2), k // 2))

    def remote(src, dst, send, recv, device):
        return pltpu.make_async_remote_copy(
            src_ref=src, dst_ref=dst, send_sem=send, recv_sem=recv,
            device_id=device, device_id_type=MESH,
        )

    my_lanes = pl.ds(pl.multiple_of(c * width, LANES), width)
    my_half = pl.ds(pl.multiple_of(c * half, half), half)
    loads = [
        pltpu.make_async_copy(hidden_hbm, hidc.at[:, my_lanes], load_sem.at[0]),
        pltpu.make_async_copy(table_hbm.at[my_half], tabc.at[:, my_lanes], load_sem.at[1]),
        pltpu.make_async_copy(table_hbm, tab, load_sem.at[2]),
    ]
    barrier = pltpu.get_barrier_semaphore()
    pl.semaphore_signal(barrier, inc=1, device_id=near, device_id_type=MESH)
    for copy in loads:
        copy.start()

    spans = {signs[way] * (b - a) for way in range(2) for b, a in tree.items()}
    heard = [
        {-b for b in range(1, half_ring + 1)} | spans,
        {b for b in range(1, half_ring)} | spans,
    ]
    heard = [sorted({offset % nz for offset in some}) for some in heard]
    for core in range(2):
        @pl.when(c == core)
        def _(core=core):
            for offset in heard[core]:
                pl.semaphore_signal(barrier, inc=1, device_id=zdev(offset), device_id_type=MESH)

    for device in cross_to:
        pl.semaphore_signal(barrier, inc=1, device_id=device, device_id_type=MESH)

    @pl.loop(1, nv)
    def _(i):
        pl.semaphore_signal(barrier, inc=1, device_id={"vocab": peer(i)}, device_id_type=MESH)

    told = jnp.where(c == 0, len(heard[0]), len(heard[1]))
    pl.semaphore_wait(barrier, told + 3 + nv - 1)

    chunk = half // CHUNKS
    gives = [remote(hidden_hbm, hidc.at[:, my_lanes], give_send.at[0], give_recv.at[0], near)]
    for j in range(CHUNKS):
        its = pl.ds(pl.multiple_of((1 - c) * half + j * chunk, chunk), chunk)
        gives.append(
            remote(
                table_hbm.at[its],
                tabc.at[pl.ds(j * chunk, chunk), my_lanes],
                give_send.at[1 + j],
                give_recv.at[1 + j],
                near,
            )
        )
    for copy in gives:
        copy.start()

    def rs_copy(way, s, g):
        rows = pl.ds(pl.multiple_of(g * 8, 8), 8)
        cols = pl.ds(0, half) if s else pl.ds(way * quarter, quarter)
        return remote(
            part.at[at_z(signs[way] * (half_ring - s)), rows, cols],
            ring.at[way, s, rows, cols],
            rs_send.at[way, min(s, 1)],
            rs_recv.at[way, s, g],
            step_to[way],
        )

    def rs_open(way):
        @pl.loop(0, groups)
        def _(g):
            rs_copy(way, 0, g).start()

    def rs_step(s):
        @pl.loop(0, groups)
        def _(g):
            rows = pl.ds(pl.multiple_of(g * 8, 8), 8)
            for way in range(2):
                cols = pl.ds(0, half) if s else pl.ds(way * quarter, quarter)
                rs_copy(way, s, g).wait_recv()
                spot = (at_z(signs[way] * (half_ring - 1 - s)), rows, cols)
                part[spot] = part[spot] + ring[way, s, rows, cols]
                rs_copy(way, s + 1, g).start()

    loads[0].wait()
    loads[1].wait()
    gives[0].wait_recv()
    for j in range(CHUNKS):
        gives[1 + j].wait_recv()
        cols = slice(j * chunk, (j + 1) * chunk)
        part[:, :, cols] = lax.dot_general(
            hidc[...], tabc[cols, :], (((1,), (1,)), ((), ())),
            preferred_element_type=jnp.float32,
        ).reshape(nz, block, chunk)
        if j == CHUNKS // 2 - 1:
            rs_open(0)
    rs_open(1)

    igs[v] = ig_ref[...].astype(jnp.float32)

    def ig_copy(i):
        return remote(igs.at[v], igs.at[v], ig_send, ig_recv, {"vocab": peer(i)})

    @pl.loop(1, nv)
    def _(i):
        ig_copy(i).start()

    def wait_ig():
        rest = igs.at[pl.ds(1, nv - 1)]
        remote(rest, rest, ig_send, ig_recv, near).wait_recv()

    piece = vocab_part // 8

    def embed(j):
        ids = owners_ref[...] * vocab_part + rows_ref[...].reshape(1, tokens) - (v * vocab_part + j * piece)
        chosen = (lax.broadcasted_iota(jnp.int32, (piece, tokens), 0) == ids).astype(jnp.float32)
        acc[pl.ds(j * piece, piece), :] = jnp.dot(
            chosen.astype(jnp.bfloat16),
            igs[...].reshape(tokens, width).astype(jnp.bfloat16),
            preferred_element_type=jnp.float32,
        )

    def own_rows():
        hid32[...] = hidc[:, my_lanes].astype(jnp.float32).reshape(nz, block, width)

    def pair_rows():
        @pl.loop(0, nz // 2)
        def _(j):
            two = jnp.concatenate([hid32[nearby(2 * j)], hid32[nearby(2 * j + 1)]], axis=0)
            rows = pl.ds(pl.multiple_of(j * 2 * block, 16), 2 * block)
            hid_near[rows, :] = two.astype(jnp.bfloat16)

    def target_columns():
        @pl.loop(0, nz)
        def _(d):
            token = lax.broadcasted_iota(jnp.int32, (block, tokens), 0) + d * block
            here = lax.broadcasted_iota(jnp.int32, (block, tokens), 1) == token
            wanted = jnp.sum(
                jnp.where(here, targets_ref[...].reshape(1, tokens).astype(jnp.float32), 0.0), axis=1, keepdims=True
            )
            tcol[d] = jnp.broadcast_to(wanted.astype(jnp.int32), (block, LANES))

    lane = lax.broadcasted_iota(jnp.int32, (1, LANES), 1)
    sub = lax.broadcasted_iota(jnp.int32, (8, LANES), 0)
    eye = lax.broadcasted_iota(jnp.int32, (block, LANES), 0) == lax.broadcasted_iota(
        jnp.int32, (block, LANES), 1
    )
    first_col = v * vocab_part

    def as_row(x):
        return jnp.sum(jnp.where(eye, x, 0.0), axis=0, keepdims=True)

    def as_col(x):
        return jnp.sum(jnp.where(eye, x, 0.0), axis=1, keepdims=True)

    st1_copy = remote(st1.at[0], st1.at[1], st1_send, st1_recv, near)

    def st2_copy(i):
        return remote(st2.at[v], st2.at[v], st2_send, st2_recv, {"vocab": peer(i)})

    below = stz.at[pl.ds(1, half_ring)]
    above = stz.at[pl.ds(half_ring + 1, half_ring - 1)]

    def stz_copy(b):
        return remote(
            stz.at[0], stz.at[c * half_ring + b], stz_send, stz_recv, zdev((1 - 2 * c) * b)
        )

    def slot_of(k):
        return jnp.where(k % 2 == 1, (k + 1) // 2, jnp.where(k == 0, 0, half_ring + k // 2))

    def pack(a, b, c):
        return jnp.where(sub == 0, a, jnp.where(sub == 1, b, c))

    def ag_copy(way, b, g):
        a = tree[b]
        d = at_z(-signs[way] * a)
        lanes = pl.ds(0, quarter)
        if b == half_ring:
            lanes = pl.ds(way * (quarter // 2), quarter // 2)
        ref = g_all.at[c, d, g, :, lanes]
        return remote(
            ref, ref, ag_send.at[way, b // half_ring], ag_recv.at[way, b - 1, g],
            zdev(signs[way] * (b - a)),
        )

    def cross_copy(way, g, side):
        lanes = pl.ds(way * (quarter // 2), quarter // 2)
        ref = g_all.at[side, at_z(-signs[way] * (half_ring - 1)), g, :, lanes]
        if side is not c:
            ref = g_all.at[side, at_z(half_ring), g, :, lanes]
        return remote(ref, ref, cross_send, cross_recv.at[way, g], cross_to[way])

    def ag_on(way, a, g):
        for b in sorted(tree):
            if tree[b] == a:
                ag_copy(way, b, g).start()
                if b == half_ring:
                    cross_copy(way, g, c).start()

    def core_copy(k, side):
        ref = g_all.at[side, nearby(k)]
        return remote(ref, ref, core_send, core_recv.at[k], near)

    def ag_step(b):
        @pl.loop(0, groups)
        def _(g):
            for way in range(2):
                ag_copy(way, b, g).wait_recv()
                ag_on(way, b, g)

        if b < half_ring:
            core_copy(2 * b - 1, c).start()
            core_copy(2 * b, c).start()

    def finish_logits():
        last = half_ring - 1

        @pl.loop(0, groups)
        def _(g):
            rows = pl.ds(pl.multiple_of(g * 8, 8), 8)
            for way in range(2):
                rs_copy(way, last, g).wait_recv()
            x = logit_scale * (part[z, rows, :] + ring[0, last, rows, :] + ring[1, last, rows, :])
            m = jnp.max(x, axis=1, keepdims=True)
            e = jnp.exp(x - m)
            g_all[c, z, g] = jnp.concatenate([e[:, :quarter], e[:, quarter:]], axis=0).astype(
                jnp.bfloat16
            )
            for way in range(2):
                ag_on(way, 0, g)
            column = lax.broadcasted_iota(jnp.int32, (8, half), 1) + (first_col + c * half)
            aimed = column == tcol[z, rows, 0:1]
            t = jnp.sum(jnp.where(aimed, x, 0.0), axis=1, keepdims=True)
            mst[rows, :] = jnp.where(
                lane == 0, m, jnp.where(lane == 1, jnp.sum(e, axis=1, keepdims=True), t)
            )

        st1[0] = pack(as_row(mst[:, 0:1]), as_row(mst[:, 1:2]), as_row(mst[:, 2:3]))
        st1_copy.start()
        core_copy(0, c).start()

    def stats_core():
        st1_copy.wait_recv()
        one, two = st1[0], st1[1]
        m1, m2 = one[0:1], two[0:1]
        m = jnp.maximum(m1, m2)
        s = one[1:2] * jnp.exp(m1 - m) + two[1:2] * jnp.exp(m2 - m)
        st2[v] = pack(m, s, one[2:3] + two[2:3])

        @pl.loop(1, nv)
        def _(i):
            st2_copy(i).start()

    def stats_final():
        rest = st2.at[pl.ds(1, nv - 1)]
        remote(rest, rest, st2_send, st2_recv, near).wait_recv()

        every = st2[...]
        m, s, t = every[:, 0], every[:, 1], every[:, 2]
        top = jnp.max(m, axis=0, keepdims=True)
        log_total = top + jnp.log(jnp.sum(s * jnp.exp(m - top), axis=0, keepdims=True))
        target = jnp.sum(t, axis=0, keepdims=True)
        mine = jnp.exp(st1[0, 0:1, :] - log_total)
        other = jnp.exp(st1[1, 0:1, :] - log_total)
        stz[0] = pack(
            jnp.where(c == 0, mine, other),
            jnp.where(c == 0, other, mine),
            jnp.exp(target - log_total) - 1.0,
        )

        @pl.loop(1, half_ring)
        def _(b):
            stz_copy(b).start()

        @pl.when(c == 0)
        def _():
            stz_copy(half_ring).start()

        pick = lax.broadcasted_iota(jnp.int32, (block, LANES), 0) == (
            lax.broadcasted_iota(jnp.int32, (block, LANES), 1) + c * (block // 2)
        )
        loss_ref[...] = jnp.broadcast_to(
            jnp.sum(jnp.where(pick, as_col(log_total - target), 0.0), axis=0, keepdims=True),
            (8, LANES),
        )

    def stz_pass():
        for core, mine in ((0, below), (1, above)):
            @pl.when(c == core)
            def _(mine=mine):
                remote(mine, mine, stz_send, stz_recv, near).wait_recv()
                remote(mine, mine, pass_send, pass_recv, near).start()

    def stz_wait():
        for core, other in ((0, above), (1, below)):
            @pl.when(c == core)
            def _(other=other):
                remote(other, other, pass_send, pass_recv, near).wait_recv()

    def core_wait(first, last):
        for k in range(first, min(last, nz - 1)):
            core_copy(k, 1 - c).wait_recv()
        if last == nz:
            @pl.loop(0, groups)
            def _(g):
                for way in range(2):
                    cross_copy(way, g, 1 - c).wait_recv()

    def gradients(first, last):
        @pl.loop(first // 2, last // 2)
        def _(j):
            rows = pl.ds(pl.multiple_of(j * 2 * block, 16), 2 * block)
            ds = [nearby(2 * j), nearby(2 * j + 1)]
            slots = [slot_of(2 * j), slot_of(2 * j + 1)]
            factors = [[as_col(stz[i, r : r + 1, :]) for r in range(3)] for i in slots]
            wanted = [tcol[d, :, 0:1] - first_col for d in ds]
            for side in range(2):
                for q in range(2):
                    base = side * half + q * quarter
                    column = lax.broadcasted_iota(jnp.int32, (block, quarter), 1) + base
                    both = []
                    for d, f, w in zip(ds, factors, wanted):
                        e = g_all[side, d].astype(jnp.float32)[:, 8 * q : 8 * q + 8, :]
                        both.append(
                            jnp.where(column == w, f[2], e.reshape(block, quarter) * f[side])
                        )
                    gn[rows, base : base + quarter] = jnp.concatenate(both, axis=0).astype(
                        jnp.bfloat16
                    )

    def hg_copy(k):
        to = nearby(k)
        return remote(
            hgs.at[k], hgr.at[v], hg_send, hg_recv, {"vocab": to}
        )

    def hidden_terms(first, last):
        if first == last:
            return
        terms = jnp.dot(
            gn[first * block : last * block, :], tab[...], preferred_element_type=jnp.float32
        ).reshape(last - first, block, width)
        tiles = [terms[:, :, i : i + LANES] for i in range(0, width, LANES)]
        rest = hgs.shape[1] - block * len(tiles)
        tiles.append(jnp.zeros((last - first, rest, LANES), jnp.float32))
        hgs[first:last] = jnp.concatenate(tiles, axis=1).astype(jnp.bfloat16)

        @pl.loop(first, last)
        def _(k):
            @pl.when(nearby(k) != v)
            def _():
                hg_copy(k).start()

    def hg_finish():
        offset = (v - z + nz + half_ring) % nz - half_ring
        k = jnp.where(offset < 0, -2 * offset - 1, 2 * offset)
        hgr[v] = hgs[k]

        rest = hgr.at[pl.ds(1, nv - 1)]
        remote(rest, rest, hg_send, hg_recv, near).wait_recv()
        total = logit_scale * jnp.sum(hgr[...].astype(jnp.float32), axis=0)
        hg_ref[...] = jnp.concatenate(
            [total[i * block : (i + 1) * block] for i in range(width // LANES)], axis=1
        ).astype(jnp.bfloat16)

    def head(j):
        spot = (pl.ds(j * piece, piece), slice(None))
        acc[spot] = acc[spot] + logit_scale * lax.dot_general(
            gn[:, j * piece : (j + 1) * piece], hid_near[...], (((0,), (0,)), ((), ())),
            preferred_element_type=jnp.float32,
        )

    def out_copy(j):
        rows = pl.ds(j * piece, piece)
        return pltpu.make_async_copy(acc.at[rows], tg_hbm.at[rows], out_sem.at[j])

    filler = [target_columns, own_rows, pair_rows, wait_ig]
    filler = filler + [functools.partial(embed, j) for j in range(8)]
    for s in range(half_ring - 1):
        rs_step(s)
        for _ in range(2):
            if filler:
                filler.pop(0)()
    while filler:
        filler.pop(0)()
    loads[2].wait()
    finish_logits()
    third = 3 * nz // 8 * 2
    stats_core()
    todo = {
        2: [stats_final],
        5: [stz_pass],
        6: [stz_wait, lambda: core_wait(0, nz // 4), lambda: gradients(0, nz // 4)],
        7: [
            lambda: core_wait(nz // 4, nz // 2),
            lambda: gradients(nz // 4, nz // 2),
            lambda: hidden_terms(0, nz // 2),
            lambda: core_wait(nz // 2, third),
            lambda: gradients(nz // 2, third),
            lambda: hidden_terms(nz // 2, third),
            lambda: core_wait(third, nz - 2),
            lambda: gradients(third, nz - 2),
        ],
    }
    for b in AG_ORDER if nz == 16 else range(1, half_ring + 1):
        ag_step(b)
        for act in todo.pop(b, []):
            act()
    for b in sorted(todo):
        for act in todo[b]:
            act()
    core_wait(nz - 2, nz)
    gradients(nz - 2, nz)
    hidden_terms(third, nz)
    for j in range(8):
        head(j)
        out_copy(j).start()
    hg_finish()

    for copy in gives:
        copy.wait_send()
    st1_copy.wait_send()

    def all_sent(ref, sem):
        remote(ref, ref, sem, sem, near).wait_send()

    for way in range(2):
        all_sent(ring.at[way, 0, :, pl.ds(0, quarter)], rs_send.at[way, 0])
        all_sent(ring.at[way, pl.ds(1, half_ring - 1)], rs_send.at[way, 1])
        all_sent(g_all.at[c, pl.ds(1, half_ring - 1)], ag_send.at[way, 0])
        all_sent(g_all.at[c, 0, :, :, pl.ds(0, quarter // 2)], ag_send.at[way, 1])
    all_sent(g_all.at[c, pl.ds(1, nz - 1)], core_send)
    all_sent(g_all.at[c, 0], cross_send)
    all_sent(igs.at[pl.ds(1, nv - 1)], ig_send)
    all_sent(st2.at[pl.ds(1, nv - 1)], st2_send)
    for core, mine in ((0, below), (1, above)):
        @pl.when(c == core)
        def _(mine=mine):
            all_sent(mine, stz_send)
            all_sent(mine, pass_send)

    all_sent(hgs.at[pl.ds(1, nv - 1)], hg_send)
    for j in range(8):
        out_copy(j).wait()


def hand_over(loss_ref, hg_in, tg_in, loss_out, hg_out, tg_out, held, in_sem, out_sem):
    def copies(j):
        spot = pl.ds(j * (tg_in.shape[0] // PIECES), tg_in.shape[0] // PIECES)
        return (
            pltpu.make_async_copy(tg_in.at[spot], held.at[spot], in_sem.at[j]),
            pltpu.make_async_copy(held.at[spot], tg_out.at[spot], out_sem.at[j]),
        )

    for j in range(PIECES):
        copies(j)[0].start()
    loss_out[...] = loss_ref[0:1, : loss_out.shape[1]]
    hg_out[...] = hg_in[...]
    for j in range(PIECES):
        copies(j)[0].wait()
        copies(j)[1].start()
    for j in range(PIECES):
        copies(j)[1].wait()


def on_device(hidden, table, targets, owners, rows, input_grad):
    nz = lax.axis_size("dp") // 2
    nv = lax.axis_size("vocab")
    tokens, width = hidden.shape
    vocab_part = table.shape[0]
    half = vocab_part // 2
    block = tokens // nz
    groups = block // 8
    half_ring = nz // 2
    packed = -(-block * (width // LANES) // 16) * 16
    f32, bf16 = jnp.float32, jnp.bfloat16
    vmem = pl.BlockSpec(memory_space=pltpu.VMEM)
    hbm = pl.BlockSpec(memory_space=pl.ANY)
    dma = pltpu.SemaphoreType.DMA
    loss, hidden_grad, table_grad = pl.pallas_call(
        functools.partial(head_kernel, nz, nv),
        out_shape=(
            jax.ShapeDtypeStruct((8, LANES), f32),
            jax.ShapeDtypeStruct((block, width), bf16),
            jax.ShapeDtypeStruct((vocab_part, width), f32),
        ),
        in_specs=[vmem, vmem, vmem, vmem, hbm, hbm],
        out_specs=(vmem, vmem, hbm),
        scratch_shapes=[
            pltpu.VMEM((tokens, 2 * width), bf16),
            pltpu.VMEM((half, 2 * width), bf16),
            pltpu.VMEM((vocab_part, width), bf16),
            pltpu.VMEM((nz, block, half), f32),
            pltpu.VMEM((2, half_ring, block, half), f32),
            pltpu.VMEM((2, nz, groups, 16, half // 2), bf16),
            pltpu.VMEM((tokens, vocab_part), bf16),
            pltpu.VMEM((vocab_part, width), f32),
            pltpu.VMEM((nz, block, width), f32),
            pltpu.VMEM((tokens, width), bf16),
            pltpu.VMEM((nz, block, LANES), jnp.int32),
            pltpu.VMEM((nz, packed, LANES), bf16),
            pltpu.VMEM((nv, packed, LANES), bf16),
            pltpu.VMEM((nv, block, width), f32),
            pltpu.VMEM((block, LANES), f32),
            pltpu.VMEM((2, 8, LANES), f32),
            pltpu.VMEM((nv, 8, LANES), f32),
            pltpu.VMEM((nz, 8, LANES), f32),
            dma((3,)),
            dma((1 + CHUNKS,)),
            dma((1 + CHUNKS,)),
            dma((2, 2)),
            dma((2, half_ring, groups)),
            dma((2, 2)),
            dma((2, half_ring, groups)),
            dma,
            dma((nz,)),
            *[dma] * 10,
            dma,
            dma((2, groups)),
            dma,
            dma,
            dma((8,)),
        ],
        compiler_params=pltpu.CompilerParams(
            collective_id=0, has_side_effects=True, vmem_limit_bytes=58 * 1024 * 1024
        ),
        name="head",
    )(
        targets, rows, owners.reshape(1, tokens),
        input_grad, hidden, table,
    )
    token_loss, hidden_grad, table_grad = pl.pallas_call(
        hand_over,
        out_shape=(
            jax.ShapeDtypeStruct((1, block // 2), f32),
            jax.ShapeDtypeStruct((block, width), bf16),
            jax.ShapeDtypeStruct((vocab_part, width), f32),
        ),
        in_specs=[vmem, vmem, hbm],
        out_specs=(vmem, vmem, hbm),
        scratch_shapes=[pltpu.VMEM((vocab_part, width), f32), dma((PIECES,)), dma((PIECES,))],
        compiler_params=pltpu.CompilerParams(vmem_limit_bytes=58 * 1024 * 1024),
        name="hand_over",
    )(loss, hidden_grad, table_grad)
    return (token_loss.reshape(block // 2), hidden_grad, table_grad)


def solution(mesh):
    return jax.shard_map(
        on_device,
        mesh=mesh,
        in_specs=(P(None, "dp"), P("vocab", "dp"), P(), P(), P(), P("vocab", "dp")),
        out_specs=(P("dp"), P("vocab", "dp"), P("vocab", "dp")),
        check_vma=False,
    )
```

```python
import functools

import jax
import jax.numpy as jnp
from jax import lax
from jax.experimental import pallas as pl
from jax.experimental.pallas import tpu as pltpu
from jax.sharding import PartitionSpec as P

logit_scale = 0.8333333
MESH = pl.DeviceIdType.MESH
LANES = 128
CHUNKS = 4
PIECES = 8
AG_TREE = {7: 5}
AG_ORDER = (1, 2, 3, 4, 5, 6, 7, 8)


def head_kernel(
    nz, nv,
    targets_hbm, rows_hbm, owners_hbm, ig_ref, hidden_hbm, table_hbm,
    loss_ref, hg_ref, tg_hbm,
    targets_ref, rows_ref, owners_ref, hidc, tabc, tab, part, ring, g_all, gn, acc, hid32, hid_near, tcol,
    hgs, hgr, igs, mst, st1, st2, stz,
    load_sem, give_send, give_recv, rs_send, rs_recv, ag_send, ag_recv, core_send, core_recv,
    st1_send, st1_recv, st2_send, st2_recv, stz_send, stz_recv, ig_send, ig_recv,
    hg_send, hg_recv, cross_send, cross_recv, pass_send, pass_recv, out_sem,
):
    half_ring = nz // 2
    tree = {b: AG_TREE.get(b, b - 1) if nz == 16 else b - 1 for b in range(1, half_ring + 1)}
    tokens, width = hidden_hbm.shape
    vocab_part = table_hbm.shape[0]
    half = vocab_part // 2
    quarter = half // 2
    block = tokens // nz
    groups = block // 8
    dp = lax.axis_index("dp")
    v = lax.axis_index("vocab")
    z = dp // 2
    c = dp % 2
    signs = (1, -1)

    def at_z(offset):
        return (z + offset + 2 * nz) % nz

    def peer(i):
        return (v + i) % nv

    def zdev(offset):
        return {"dp": at_z(offset) * 2 + c}

    near = {"dp": z * 2 + (1 - c)}
    step_to = tuple(zdev(sign) for sign in signs)
    cross_to = tuple({"dp": at_z(sign) * 2 + (1 - c)} for sign in signs)

    def nearby(k):
        return at_z(jnp.where(k % 2 == 1, -((k + 1) // 2), k // 2))

    def remote(src, dst, send, recv, device):
        return pltpu.make_async_remote_copy(
            src_ref=src, dst_ref=dst, send_sem=send, recv_sem=recv,
            device_id=device, device_id_type=MESH,
        )

    my_lanes = pl.ds(pl.multiple_of(c * width, LANES), width)
    my_half = pl.ds(pl.multiple_of(c * half, half), half)
    loads = [
        pltpu.make_async_copy(hidden_hbm, hidc.at[:, my_lanes], load_sem.at[0]),
        pltpu.make_async_copy(table_hbm.at[my_half], tabc.at[:, my_lanes], load_sem.at[1]),
        pltpu.make_async_copy(table_hbm, tab, load_sem.at[2]),
        pltpu.make_async_copy(targets_hbm, targets_ref, load_sem.at[3]),
        pltpu.make_async_copy(rows_hbm, rows_ref, load_sem.at[4]),
        pltpu.make_async_copy(owners_hbm, owners_ref, load_sem.at[5]),
    ]
    barrier = pltpu.get_barrier_semaphore()
    pl.semaphore_signal(barrier, inc=1, device_id=near, device_id_type=MESH)

    spans = {signs[way] * (b - a) for way in range(2) for b, a in tree.items()}
    heard = [
        {-b for b in range(1, half_ring + 1)} | spans,
        {b for b in range(1, half_ring)} | spans,
    ]
    heard = [sorted({offset % nz for offset in some}) for some in heard]
    for core in range(2):
        @pl.when(c == core)
        def _(core=core):
            for offset in heard[core]:
                pl.semaphore_signal(barrier, inc=1, device_id=zdev(offset), device_id_type=MESH)

    for device in cross_to:
        pl.semaphore_signal(barrier, inc=1, device_id=device, device_id_type=MESH)

    @pl.loop(1, nv)
    def _(i):
        pl.semaphore_signal(barrier, inc=1, device_id={"vocab": peer(i)}, device_id_type=MESH)

    for copy in loads:
        copy.start()
    told = jnp.where(c == 0, len(heard[0]), len(heard[1]))
    pl.semaphore_wait(barrier, told + 3 + nv - 1)

    chunk = half // CHUNKS
    gives = [remote(hidden_hbm, hidc.at[:, my_lanes], give_send.at[0], give_recv.at[0], near)]
    for j in range(CHUNKS):
        its = pl.ds(pl.multiple_of((1 - c) * half + j * chunk, chunk), chunk)
        gives.append(
            remote(
                table_hbm.at[its],
                tabc.at[pl.ds(j * chunk, chunk), my_lanes],
                give_send.at[1 + j],
                give_recv.at[1 + j],
                near,
            )
        )
    for copy in gives:
        copy.start()

    def rs_copy(way, s, g):
        rows = pl.ds(pl.multiple_of(g * 8, 8), 8)
        cols = pl.ds(0, half) if s else pl.ds(way * quarter, quarter)
        return remote(
            part.at[at_z(signs[way] * (half_ring - s)), rows, cols],
            ring.at[way, s, rows, cols],
            rs_send.at[way, min(s, 1)],
            rs_recv.at[way, s, g],
            step_to[way],
        )

    def rs_open(way):
        @pl.loop(0, groups)
        def _(g):
            rs_copy(way, 0, g).start()

    def rs_step(s):
        @pl.loop(0, groups)
        def _(g):
            rows = pl.ds(pl.multiple_of(g * 8, 8), 8)
            for way in range(2):
                cols = pl.ds(0, half) if s else pl.ds(way * quarter, quarter)
                rs_copy(way, s, g).wait_recv()
                spot = (at_z(signs[way] * (half_ring - 1 - s)), rows, cols)
                part[spot] = part[spot] + ring[way, s, rows, cols]
                rs_copy(way, s + 1, g).start()

    loads[0].wait()
    loads[1].wait()
    gives[0].wait_recv()
    for j in range(CHUNKS):
        gives[1 + j].wait_recv()
        cols = slice(j * chunk, (j + 1) * chunk)
        part[:, :, cols] = lax.dot_general(
            hidc[...], tabc[cols, :], (((1,), (1,)), ((), ())),
            preferred_element_type=jnp.float32,
        ).reshape(nz, block, chunk)
        if j == CHUNKS // 2 - 1:
            rs_open(0)
    rs_open(1)

    for copy in loads[3:]:
        copy.wait()
    igs[v] = ig_ref[...].astype(jnp.float32)

    def ig_copy(i):
        return remote(igs.at[v], igs.at[v], ig_send, ig_recv, {"vocab": peer(i)})

    @pl.loop(1, nv)
    def _(i):
        ig_copy(i).start()

    def wait_ig():
        rest = igs.at[pl.ds(1, nv - 1)]
        remote(rest, rest, ig_send, ig_recv, near).wait_recv()

    piece = vocab_part // 8

    def embed(j):
        ids = owners_ref[...] * vocab_part + rows_ref[...].reshape(1, tokens) - (v * vocab_part + j * piece)
        chosen = (lax.broadcasted_iota(jnp.int32, (piece, tokens), 0) == ids).astype(jnp.float32)
        acc[pl.ds(j * piece, piece), :] = jnp.dot(
            chosen.astype(jnp.bfloat16),
            igs[...].reshape(tokens, width).astype(jnp.bfloat16),
            preferred_element_type=jnp.float32,
        )

    def own_rows():
        hid32[...] = hidc[:, my_lanes].astype(jnp.float32).reshape(nz, block, width)

    def pair_rows():
        @pl.loop(0, nz // 2)
        def _(j):
            two = jnp.concatenate([hid32[nearby(2 * j)], hid32[nearby(2 * j + 1)]], axis=0)
            rows = pl.ds(pl.multiple_of(j * 2 * block, 16), 2 * block)
            hid_near[rows, :] = two.astype(jnp.bfloat16)

    def target_columns():
        @pl.loop(0, nz)
        def _(d):
            token = lax.broadcasted_iota(jnp.int32, (block, tokens), 0) + d * block
            here = lax.broadcasted_iota(jnp.int32, (block, tokens), 1) == token
            wanted = jnp.sum(
                jnp.where(here, targets_ref[...].reshape(1, tokens).astype(jnp.float32), 0.0), axis=1, keepdims=True
            )
            tcol[d] = jnp.broadcast_to(wanted.astype(jnp.int32), (block, LANES))

    lane = lax.broadcasted_iota(jnp.int32, (1, LANES), 1)
    sub = lax.broadcasted_iota(jnp.int32, (8, LANES), 0)
    eye = lax.broadcasted_iota(jnp.int32, (block, LANES), 0) == lax.broadcasted_iota(
        jnp.int32, (block, LANES), 1
    )
    first_col = v * vocab_part

    def as_row(x):
        return jnp.sum(jnp.where(eye, x, 0.0), axis=0, keepdims=True)

    def as_col(x):
        return jnp.sum(jnp.where(eye, x, 0.0), axis=1, keepdims=True)

    st1_copy = remote(st1.at[0], st1.at[1], st1_send, st1_recv, near)

    def st2_copy(i):
        return remote(st2.at[v], st2.at[v], st2_send, st2_recv, {"vocab": peer(i)})

    below = stz.at[pl.ds(1, half_ring)]
    above = stz.at[pl.ds(half_ring + 1, half_ring - 1)]

    def stz_copy(b):
        return remote(
            stz.at[0], stz.at[c * half_ring + b], stz_send, stz_recv, zdev((1 - 2 * c) * b)
        )

    def slot_of(k):
        return jnp.where(k % 2 == 1, (k + 1) // 2, jnp.where(k == 0, 0, half_ring + k // 2))

    def pack(a, b, c):
        return jnp.where(sub == 0, a, jnp.where(sub == 1, b, c))

    def ag_copy(way, b, g):
        a = tree[b]
        d = at_z(-signs[way] * a)
        lanes = pl.ds(0, quarter)
        if b == half_ring:
            lanes = pl.ds(way * (quarter // 2), quarter // 2)
        ref = g_all.at[c, d, g, :, lanes]
        return remote(
            ref, ref, ag_send.at[way, b // half_ring], ag_recv.at[way, b - 1, g],
            zdev(signs[way] * (b - a)),
        )

    def cross_copy(way, g, side):
        lanes = pl.ds(way * (quarter // 2), quarter // 2)
        ref = g_all.at[side, at_z(-signs[way] * (half_ring - 1)), g, :, lanes]
        if side is not c:
            ref = g_all.at[side, at_z(half_ring), g, :, lanes]
        return remote(ref, ref, cross_send, cross_recv.at[way, g], cross_to[way])

    def ag_on(way, a, g):
        for b in sorted(tree):
            if tree[b] == a:
                ag_copy(way, b, g).start()
                if b == half_ring:
                    cross_copy(way, g, c).start()

    def core_copy(k, side):
        ref = g_all.at[side, nearby(k)]
        return remote(ref, ref, core_send, core_recv.at[k], near)

    def ag_step(b):
        @pl.loop(0, groups)
        def _(g):
            for way in range(2):
                ag_copy(way, b, g).wait_recv()
                ag_on(way, b, g)

        if b < half_ring:
            core_copy(2 * b - 1, c).start()
            core_copy(2 * b, c).start()

    def finish_logits():
        last = half_ring - 1

        @pl.loop(0, groups)
        def _(g):
            rows = pl.ds(pl.multiple_of(g * 8, 8), 8)
            for way in range(2):
                rs_copy(way, last, g).wait_recv()
            x = logit_scale * (part[z, rows, :] + ring[0, last, rows, :] + ring[1, last, rows, :])
            m = jnp.max(x, axis=1, keepdims=True)
            e = jnp.exp(x - m)
            g_all[c, z, g] = jnp.concatenate([e[:, :quarter], e[:, quarter:]], axis=0).astype(
                jnp.bfloat16
            )
            for way in range(2):
                ag_on(way, 0, g)
            column = lax.broadcasted_iota(jnp.int32, (8, half), 1) + (first_col + c * half)
            aimed = column == tcol[z, rows, 0:1]
            t = jnp.sum(jnp.where(aimed, x, 0.0), axis=1, keepdims=True)
            mst[rows, :] = jnp.where(
                lane == 0, m, jnp.where(lane == 1, jnp.sum(e, axis=1, keepdims=True), t)
            )

        st1[0] = pack(as_row(mst[:, 0:1]), as_row(mst[:, 1:2]), as_row(mst[:, 2:3]))
        st1_copy.start()
        core_copy(0, c).start()

    def stats_core():
        st1_copy.wait_recv()
        one, two = st1[0], st1[1]
        m1, m2 = one[0:1], two[0:1]
        m = jnp.maximum(m1, m2)
        s = one[1:2] * jnp.exp(m1 - m) + two[1:2] * jnp.exp(m2 - m)
        st2[v] = pack(m, s, one[2:3] + two[2:3])

        @pl.loop(1, nv)
        def _(i):
            st2_copy(i).start()

    def stats_final():
        rest = st2.at[pl.ds(1, nv - 1)]
        remote(rest, rest, st2_send, st2_recv, near).wait_recv()

        every = st2[...]
        m, s, t = every[:, 0], every[:, 1], every[:, 2]
        top = jnp.max(m, axis=0, keepdims=True)
        log_total = top + jnp.log(jnp.sum(s * jnp.exp(m - top), axis=0, keepdims=True))
        target = jnp.sum(t, axis=0, keepdims=True)
        mine = jnp.exp(st1[0, 0:1, :] - log_total)
        other = jnp.exp(st1[1, 0:1, :] - log_total)
        stz[0] = pack(
            jnp.where(c == 0, mine, other),
            jnp.where(c == 0, other, mine),
            jnp.exp(target - log_total) - 1.0,
        )

        @pl.loop(1, half_ring)
        def _(b):
            stz_copy(b).start()

        @pl.when(c == 0)
        def _():
            stz_copy(half_ring).start()

        pick = lax.broadcasted_iota(jnp.int32, (block, LANES), 0) == (
            lax.broadcasted_iota(jnp.int32, (block, LANES), 1) + c * (block // 2)
        )
        loss_ref[...] = jnp.broadcast_to(
            jnp.sum(jnp.where(pick, as_col(log_total - target), 0.0), axis=0, keepdims=True),
            (8, LANES),
        )

    def stz_pass():
        for core, mine in ((0, below), (1, above)):
            @pl.when(c == core)
            def _(mine=mine):
                remote(mine, mine, stz_send, stz_recv, near).wait_recv()
                remote(mine, mine, pass_send, pass_recv, near).start()

    def stz_wait():
        for core, other in ((0, above), (1, below)):
            @pl.when(c == core)
            def _(other=other):
                remote(other, other, pass_send, pass_recv, near).wait_recv()

    def core_wait(first, last):
        for k in range(first, min(last, nz - 1)):
            core_copy(k, 1 - c).wait_recv()
        if last == nz:
            @pl.loop(0, groups)
            def _(g):
                for way in range(2):
                    cross_copy(way, g, 1 - c).wait_recv()

    def gradients(first, last):
        @pl.loop(first // 2, last // 2)
        def _(j):
            rows = pl.ds(pl.multiple_of(j * 2 * block, 16), 2 * block)
            ds = [nearby(2 * j), nearby(2 * j + 1)]
            slots = [slot_of(2 * j), slot_of(2 * j + 1)]
            factors = [[as_col(stz[i, r : r + 1, :]) for r in range(3)] for i in slots]
            wanted = [tcol[d, :, 0:1] - first_col for d in ds]
            for side in range(2):
                for q in range(2):
                    base = side * half + q * quarter
                    column = lax.broadcasted_iota(jnp.int32, (block, quarter), 1) + base
                    both = []
                    for d, f, w in zip(ds, factors, wanted):
                        e = g_all[side, d].astype(jnp.float32)[:, 8 * q : 8 * q + 8, :]
                        both.append(
                            jnp.where(column == w, f[2], e.reshape(block, quarter) * f[side])
                        )
                    gn[rows, base : base + quarter] = jnp.concatenate(both, axis=0).astype(
                        jnp.bfloat16
                    )

    def hg_copy(k):
        to = nearby(k)
        return remote(
            hgs.at[k], hgr.at[v], hg_send, hg_recv, {"vocab": to}
        )

    def hidden_terms(first, last):
        if first == last:
            return
        terms = jnp.dot(
            gn[first * block : last * block, :], tab[...], preferred_element_type=jnp.float32
        ).reshape(last - first, block, width)
        tiles = [terms[:, :, i : i + LANES] for i in range(0, width, LANES)]
        rest = hgs.shape[1] - block * len(tiles)
        tiles.append(jnp.zeros((last - first, rest, LANES), jnp.float32))
        hgs[first:last] = jnp.concatenate(tiles, axis=1).astype(jnp.bfloat16)

        @pl.loop(first, last)
        def _(k):
            @pl.when(nearby(k) != v)
            def _():
                hg_copy(k).start()

    def hg_finish():
        offset = (v - z + nz + half_ring) % nz - half_ring
        k = jnp.where(offset < 0, -2 * offset - 1, 2 * offset)
        hgr[v] = hgs[k]

        rest = hgr.at[pl.ds(1, nv - 1)]
        remote(rest, rest, hg_send, hg_recv, near).wait_recv()
        total = logit_scale * jnp.sum(hgr[...].astype(jnp.float32), axis=0)
        hg_ref[...] = jnp.concatenate(
            [total[i * block : (i + 1) * block] for i in range(width // LANES)], axis=1
        )

    def head(j):
        spot = (pl.ds(j * piece, piece), slice(None))
        acc[spot] = acc[spot] + logit_scale * lax.dot_general(
            gn[:, j * piece : (j + 1) * piece], hid_near[...], (((0,), (0,)), ((), ())),
            preferred_element_type=jnp.float32,
        )

    def out_copy(j):
        rows = pl.ds(j * piece, piece)
        return pltpu.make_async_copy(acc.at[rows], tg_hbm.at[rows], out_sem.at[j])

    filler = [target_columns, own_rows, pair_rows, wait_ig]
    filler = filler + [functools.partial(embed, j) for j in range(8)]
    for s in range(half_ring - 1):
        rs_step(s)
        for _ in range(2):
            if filler:
                filler.pop(0)()
    while filler:
        filler.pop(0)()
    loads[2].wait()
    finish_logits()
    third = 3 * nz // 8 * 2
    stats_core()
    todo = {
        3: [stats_final],
        5: [stz_pass],
        6: [stz_wait, lambda: core_wait(0, nz // 4), lambda: gradients(0, nz // 4)],
        7: [
            lambda: core_wait(nz // 4, nz // 2),
            lambda: gradients(nz // 4, nz // 2),
            lambda: hidden_terms(0, nz // 2),
            lambda: core_wait(nz // 2, third),
            lambda: gradients(nz // 2, third),
            lambda: hidden_terms(nz // 2, third),
            lambda: core_wait(third, nz - 2),
            lambda: gradients(third, nz - 2),
        ],
    }
    for b in AG_ORDER if nz == 16 else range(1, half_ring + 1):
        ag_step(b)
        for act in todo.pop(b, []):
            act()
    for b in sorted(todo):
        for act in todo[b]:
            act()
    core_wait(nz - 2, nz)
    gradients(nz - 2, nz)
    hidden_terms(third, nz)
    for j in range(8):
        head(j)
        out_copy(j).start()
    hg_finish()

    for copy in gives:
        copy.wait_send()
    st1_copy.wait_send()

    def all_sent(ref, sem):
        remote(ref, ref, sem, sem, near).wait_send()

    for way in range(2):
        all_sent(ring.at[way, 0, :, pl.ds(0, quarter)], rs_send.at[way, 0])
        all_sent(ring.at[way, pl.ds(1, half_ring - 1)], rs_send.at[way, 1])
        all_sent(g_all.at[c, pl.ds(1, half_ring - 1)], ag_send.at[way, 0])
        all_sent(g_all.at[c, 0, :, :, pl.ds(0, quarter // 2)], ag_send.at[way, 1])
    all_sent(g_all.at[c, pl.ds(1, nz - 1)], core_send)
    all_sent(g_all.at[c, 0], cross_send)
    all_sent(igs.at[pl.ds(1, nv - 1)], ig_send)
    all_sent(st2.at[pl.ds(1, nv - 1)], st2_send)
    for core, mine in ((0, below), (1, above)):
        @pl.when(c == core)
        def _(mine=mine):
            all_sent(mine, stz_send)
            all_sent(mine, pass_send)

    all_sent(hgs.at[pl.ds(1, nv - 1)], hg_send)
    for j in range(8):
        out_copy(j).wait()


def hand_over(
    loss_in, hg_in, tg_in, loss_out, hg_out, tg_out, loss_ref, hg_ref, held, small_sem, in_sem, out_sem
):
    def copies(j):
        spot = pl.ds(j * (tg_in.shape[0] // PIECES), tg_in.shape[0] // PIECES)
        return (
            pltpu.make_async_copy(tg_in.at[spot], held.at[spot], in_sem.at[j]),
            pltpu.make_async_copy(held.at[spot], tg_out.at[spot], out_sem.at[j]),
        )

    small = [
        pltpu.make_async_copy(loss_in, loss_ref, small_sem.at[0]),
        pltpu.make_async_copy(hg_in, hg_ref, small_sem.at[1]),
    ]
    for copy in small:
        copy.start()
    for j in range(PIECES):
        copies(j)[0].start()
    for j in range(PIECES):
        copies(j)[0].wait()
        copies(j)[1].start()
    for copy in small:
        copy.wait()
    loss_out[...] = loss_ref[0:1, : loss_out.shape[1]]
    hg_out[...] = hg_ref[...].astype(jnp.bfloat16)
    for j in range(PIECES):
        copies(j)[1].wait()


def on_device(hidden, table, targets, owners, rows, input_grad):
    nz = lax.axis_size("dp") // 2
    nv = lax.axis_size("vocab")
    tokens, width = hidden.shape
    vocab_part = table.shape[0]
    half = vocab_part // 2
    block = tokens // nz
    groups = block // 8
    half_ring = nz // 2
    packed = -(-block * (width // LANES) // 16) * 16
    f32, bf16 = jnp.float32, jnp.bfloat16
    vmem = pl.BlockSpec(memory_space=pltpu.VMEM)
    hbm = pl.BlockSpec(memory_space=pl.ANY)
    dma = pltpu.SemaphoreType.DMA
    loss, hidden_grad, table_grad = pl.pallas_call(
        functools.partial(head_kernel, nz, nv),
        out_shape=(
            jax.ShapeDtypeStruct((8, LANES), f32),
            jax.ShapeDtypeStruct((block, width), f32),
            jax.ShapeDtypeStruct((vocab_part, width), f32),
        ),
        in_specs=[hbm, hbm, hbm, vmem, hbm, hbm],
        out_specs=(vmem, vmem, hbm),
        scratch_shapes=[
            pltpu.VMEM((tokens,), jnp.int32),
            pltpu.VMEM((tokens,), jnp.int32),
            pltpu.VMEM((1, tokens), jnp.int32),
            pltpu.VMEM((tokens, 2 * width), bf16),
            pltpu.VMEM((half, 2 * width), bf16),
            pltpu.VMEM((vocab_part, width), bf16),
            pltpu.VMEM((nz, block, half), f32),
            pltpu.VMEM((2, half_ring, block, half), f32),
            pltpu.VMEM((2, nz, groups, 16, half // 2), bf16),
            pltpu.VMEM((tokens, vocab_part), bf16),
            pltpu.VMEM((vocab_part, width), f32),
            pltpu.VMEM((nz, block, width), f32),
            pltpu.VMEM((tokens, width), bf16),
            pltpu.VMEM((nz, block, LANES), jnp.int32),
            pltpu.VMEM((nz, packed, LANES), bf16),
            pltpu.VMEM((nv, packed, LANES), bf16),
            pltpu.VMEM((nv, block, width), f32),
            pltpu.VMEM((block, LANES), f32),
            pltpu.VMEM((2, 8, LANES), f32),
            pltpu.VMEM((nv, 8, LANES), f32),
            pltpu.VMEM((nz, 8, LANES), f32),
            dma((6,)),
            dma((1 + CHUNKS,)),
            dma((1 + CHUNKS,)),
            dma((2, 2)),
            dma((2, half_ring, groups)),
            dma((2, 2)),
            dma((2, half_ring, groups)),
            dma,
            dma((nz,)),
            *[dma] * 10,
            dma,
            dma((2, groups)),
            dma,
            dma,
            dma((8,)),
        ],
        compiler_params=pltpu.CompilerParams(
            collective_id=0, has_side_effects=True, vmem_limit_bytes=58 * 1024 * 1024
        ),
        name="head",
    )(
        targets, rows, owners.reshape(1, tokens),
        input_grad, hidden, table,
    )
    token_loss, hidden_grad, table_grad = pl.pallas_call(
        hand_over,
        out_shape=(
            jax.ShapeDtypeStruct((1, block // 2), f32),
            jax.ShapeDtypeStruct((block, width), bf16),
            jax.ShapeDtypeStruct((vocab_part, width), f32),
        ),
        in_specs=[hbm] * 3,
        out_specs=(vmem, vmem, hbm),
        scratch_shapes=[
            pltpu.VMEM((8, LANES), f32),
            pltpu.VMEM((block, width), f32),
            pltpu.VMEM((vocab_part, width), f32),
            dma((2,)),
            dma((PIECES,)),
            dma((PIECES,)),
        ],
        compiler_params=pltpu.CompilerParams(vmem_limit_bytes=58 * 1024 * 1024),
        name="hand_over",
    )(loss, hidden_grad, table_grad)
    return (token_loss.reshape(block // 2), hidden_grad, table_grad)


def solution(mesh):
    return jax.shard_map(
        on_device,
        mesh=mesh,
        in_specs=(P(None, "dp"), P("vocab", "dp"), P(), P(), P(), P("vocab", "dp")),
        out_specs=(P("dp"), P("vocab", "dp"), P("vocab", "dp")),
        check_vma=False,
    )
```
